128 devices in a mesh: row: 16 (over y, x), col: 8 (over z, core).
Axes of the slice: x: 4, y: 4, z: 4, core: 2. Of those that a mesh axis runs over, the one named last changes fastest.
Arguments:
- object_field: float32 [2, 8192, 4096], P(None, 'row', 'col'), may hold values from -6 to 6
- probe: float32 [2, 256, 256], replicated, may hold values from -6 to 6
- amplitude: float32 [16, 8, 4, 256, 256], P('row', 'col'), may hold values from 0.1 to 3
- positions: int32 [16, 8, 4, 2], P('row', 'col'), may hold values from 0 to 511
- counts: int32 [16, 8], P('row', 'col'), may hold values from 1 to 4, as said below
Outputs:
- object_out: float32 [2, 8192, 4096], P(None, 'row', 'col')
- probe_out: float32 [2, 256, 256], replicated
The draws below stay inside these ranges and needn't reach their ends.
Inputs may be any that keep to these rules, and one draw needn't show every extreme that they name: `counts`: every device has 1 to 4 live slots, its first ones; some device has 4 in every draw and about a quarter have 4, the rest at most half of it.
All inputs are finite; a program needn't handle non-finite values.
Results may differ from the reference program's by a relative error of at most 0.0003.
Values sent between devices are 32-bit elements; how exact they have to be, the bound alone decides.
No kernel may reach another device: no remote copies, remote signals or barrier semaphores. Data moves between devices by JAX's collectives and lax.ppermute only.
A program may use at most 128 MiB of HBM per device.

```python
import math
import jax
import jax.numpy as jnp
from jax import lax

F = 256
TILE = 512
P_MAX = 4
PASSES = 3
GRID_R = 16
GRID_C = 8
NR = 8192
NC = 4096


def draw_counts(key, part):
    key = jax.random.fold_in(key, 7)
    first, second, third = jax.random.split(key, 3)
    heavy = jax.random.randint(first, (GRID_R, GRID_C), 0, 4) == 0
    lighter = jax.random.randint(second, (GRID_R, GRID_C), 1, P_MAX // 2 + 1)
    counts = jnp.where(heavy, P_MAX, lighter).astype(jnp.int32).reshape(-1)
    chosen = jax.random.randint(third, (), 0, GRID_R * GRID_C)
    counts = counts.at[chosen].set(P_MAX)
    return counts.reshape(GRID_R, GRID_C).astype(jnp.int32)


def place_ends(result, key, least, top_value):
    longest = result.shape.index(max(result.shape))
    spots = []
    for shift in (0, 1):
        where = [jax.random.randint(jax.random.fold_in(key, axis), (), 0, length) for axis, length in enumerate(result.shape)]
        where[longest] = (where[longest] + shift) % result.shape[longest]
        spots.append(tuple(where))
    return result.at[spots[0]].set(least).at[spots[1]].set(top_value)


def block_scale(own_key, shape, cuts, smallest, largest):
    factor_of = 1.0
    for dim, blocks in cuts:
        steps = jax.random.uniform(jax.random.fold_in(jax.random.fold_in(own_key, 6), dim), (blocks,), jnp.float32, smallest / len(cuts), largest / len(cuts))
        factor_of = factor_of * jnp.repeat(jnp.exp(steps), shape[dim] // blocks).reshape((-1,) + (1,) * (len(shape) - 1 - dim))
    return factor_of


def noise(key, dims, width, most, pieces=(), kind=jnp.bfloat16):
    result = jax.random.normal(key, dims, jnp.float32) * width
    if len(pieces) > 0:
        result = block_scale(key, dims, pieces, -0.22, 0.18) * result
    return jnp.clip(result, min=-most, max=most).astype(kind)


def setup_inputs(seed: int = 0) -> dict:
    key_of = jax.random.split(jax.random.key(seed), 6)
    return {
        "object_field": noise(key_of[0], (2, NR, NC), 1.0, 6.0, ((1, 16), (2, 8)), jnp.float32),
        "probe": noise(key_of[1], (2, F, F), 1.0, 6.0, (), jnp.float32),
        "amplitude": jnp.clip(jnp.exp(math.log(3.0) - 3.4011974 * jax.random.uniform(key_of[2], (GRID_R, GRID_C, P_MAX, F, F), jnp.float32) ** block_scale(key_of[2], (GRID_R, GRID_C, P_MAX, F, F), ((0, 16), (1, 8)), -0.2, 0.2)), 0.1, 3.0),
        "positions": place_ends(jax.random.randint(key_of[3], (GRID_R, GRID_C, P_MAX, 2), 0, TILE), jax.random.fold_in(key_of[3], 1), 0, TILE - 1).astype(jnp.int32),
        "counts": draw_counts(jax.random.fold_in(key_of[5], 71), 0),
    }


amp_floor = 0.1
object_damping = 0.5
probe_damping = 1.0


def reference(object_field, probe, amplitude, positions, counts):
    rows_all = GRID_R * TILE
    cols_all = GRID_C * TILE
    base_rows = jnp.arange(GRID_R, dtype=jnp.int32)[:, None, None] * TILE
    base_cols = jnp.arange(GRID_C, dtype=jnp.int32)[None, :, None] * TILE
    glob_rows = (positions[..., 0] + base_rows).reshape(-1).astype(jnp.int32)
    glob_cols = (positions[..., 1] + base_cols).reshape(-1).astype(jnp.int32)
    active = (jnp.arange(P_MAX, dtype=jnp.int32)[None, None, :] < counts[:, :, None]).astype(jnp.float32).reshape(-1)
    measured = amplitude.reshape(-1, F, F)
    estimate = object_field
    probe_now = probe
    for sweep_index in range(PASSES):
        extended = jnp.concatenate([estimate, estimate[:, :F, :]], axis=1)
        extended = jnp.concatenate([extended, extended[:, :, :F]], axis=2)
        probe_cplx = probe_now[0] + 1j * probe_now[1]

        def visit_slot(totals, sample):
            canvas, grad_re, grad_im, power_sum = totals
            row_at, col_at, measure, weight = sample
            row_at = row_at.astype(jnp.int32)
            col_at = col_at.astype(jnp.int32)
            anchor = jnp.zeros((), jnp.int32)
            patch_field = lax.dynamic_slice(extended, (anchor, row_at, col_at), (2, F, F))
            patch_cplx = patch_field[0] + 1j * patch_field[1]
            far_field = jnp.fft.fft2(probe_cplx * patch_cplx, norm="ortho")
            modulus = jnp.abs(far_field)
            difference = far_field * (measure / jnp.maximum(modulus, amp_floor) - 1.0)
            correction = jnp.fft.ifft2(difference, norm="ortho") * weight
            update = jnp.conj(probe_cplx) * correction
            contribution = jnp.stack([update.real, update.imag, (probe_now[0] ** 2 + probe_now[1] ** 2) * weight])
            current = lax.dynamic_slice(canvas, (anchor, row_at, col_at), (3, F, F))
            canvas = lax.dynamic_update_slice(canvas, current + contribution, (anchor, row_at, col_at))
            probe_term = jnp.conj(patch_cplx) * correction
            power_sum = power_sum + (patch_field[0] ** 2 + patch_field[1] ** 2) * weight
            return (canvas, grad_re + probe_term.real, grad_im + probe_term.imag, power_sum), None

        initial = (jnp.zeros((3, rows_all + F, cols_all + F), jnp.float32), jnp.zeros((F, F), jnp.float32), jnp.zeros((F, F), jnp.float32), jnp.zeros((F, F), jnp.float32))
        (canvas, grad_re, grad_im, power_sum), unused = lax.scan(visit_slot, initial, (glob_rows, glob_cols, measured, active))
        folded = canvas[:, :rows_all, :cols_all]
        folded = folded.at[:, :F, :].add(canvas[:, rows_all:, :cols_all])
        folded = folded.at[:, :, :F].add(canvas[:, :rows_all, cols_all:])
        folded = folded.at[:, :F, :F].add(canvas[:, rows_all:, cols_all:])
        estimate = estimate + folded[:2] / (folded[2] + object_damping)
        probe_now = probe_now + jnp.stack([grad_re, grad_im]) / (power_sum + probe_damping)
    return estimate, probe_now
```

```python
import math

import jax
import jax.numpy as jnp
import numpy as np
from jax import lax
from jax.experimental import pallas as pl
from jax.experimental.pallas import tpu as pltpu
from jax.sharding import PartitionSpec as P

PASSES = 3
F = 256
TILE = 512
WIDE = TILE + F
HALF = F // 2
LANES = 128

amp_floor = 0.1
object_damping = 0.5
probe_damping = 1.0

VMEM = pl.BlockSpec(memory_space=pltpu.VMEM)
SMEM = pl.BlockSpec(memory_space=pltpu.SMEM)


def passed_along(block, axis, distance):
    size = lax.axis_size(axis)
    route = [((i - distance) % size, i) for i in range(size)]
    return lax.ppermute(block, axis, route)


def split(x):
    high = x.astype(jnp.bfloat16)
    low = (x - high.astype(jnp.float32)).astype(jnp.bfloat16)
    return high, low


def tables():
    k = np.arange(F)
    angles = (k[:, None] * k[None, :] % F) * (-2.0 * math.pi / F)
    re = np.cos(angles) / math.sqrt(F)
    im = np.sin(angles) / math.sqrt(F)
    left = np.block([[re, -im], [im, re]]).astype(np.float32)
    right = np.block([[re, im], [-im, re]]).astype(np.float32)

    def terms(m):
        high = m.astype(jnp.bfloat16)
        low = (m - high.astype(np.float32)).astype(jnp.bfloat16)
        return high, low

    lh, ll = terms(left)
    rh, rl = terms(right)
    return np.concatenate([lh, lh, ll], 1), np.concatenate([rh, rh, rl], 0)


def transform(re, im, left, right):
    h, l = split(jnp.concatenate([re, im], 0))
    y = jnp.dot(left[...], jnp.concatenate([h, l, h], 0), preferred_element_type=jnp.float32)
    h, l = split(jnp.concatenate([y[:F], y[F:]], 1))
    z = jnp.dot(jnp.concatenate([h, l, h], 1), right[...], preferred_element_type=jnp.float32)
    return z[:, :F], z[:, F:]


def window(ref, lead, r, c):
    r0 = pl.multiple_of((r // 8) * 8, 8)
    c0 = pl.multiple_of((c // LANES) * LANES, LANES)
    rs, cs = r - r0, c - c0
    w = ref[lead + (pl.ds(r0, F + 8), pl.ds(c0, F + LANES))]
    lane = lax.broadcasted_iota(jnp.int32, (F + 8, LANES), 1)
    back = lax.rem(LANES - cs, LANES)
    t = [pltpu.roll(w[:, i * LANES : (i + 1) * LANES], back, 1) for i in range(3)]
    w = jnp.concatenate([jnp.where(lane < LANES - cs, t[i], t[i + 1]) for i in range(2)], 1)
    w = pltpu.roll(w.reshape(F // 8 + 1, 8, F), lax.rem(8 - rs, 8), 1)
    sub = lax.broadcasted_iota(jnp.int32, (F // 8, 8, F), 1)
    return jnp.where(sub < 8 - rs, w[:-1], w[1:]).reshape(F, F)


def deposit(ref, lead, r, c, x):
    r0 = pl.multiple_of((r // 8) * 8, 8)
    c0 = pl.multiple_of((c // LANES) * LANES, LANES)
    rs, cs = r - r0, c - c0
    w = pltpu.roll(x.reshape(F // 8, 8, F), rs, 1)
    zero = jnp.zeros((1, 8, F), jnp.float32)
    sub = lax.broadcasted_iota(jnp.int32, (F // 8 + 1, 8, F), 1)
    w = jnp.where(sub >= rs, jnp.concatenate([w, zero], 0), jnp.concatenate([zero, w], 0))
    w = w.reshape(F + 8, F)
    lane = lax.broadcasted_iota(jnp.int32, (F + 8, LANES), 1)
    a = pltpu.roll(w[:, :LANES], cs, 1)
    b = pltpu.roll(w[:, LANES:], cs, 1)
    t = [jnp.where(lane >= cs, a, 0.0), jnp.where(lane >= cs, b, a), jnp.where(lane >= cs, 0.0, b)]
    at = lead + (pl.ds(r0, F + 8), pl.ds(c0, F + LANES))
    ref[at] = ref[at] + jnp.concatenate(t, 1)


def visit_frames(info, amplitude, left, right, ob, pr, canvas, glow, grads):
    canvas[...] = jnp.zeros_like(canvas)
    glow[F : F + WIDE, F : F + WIDE] = jnp.zeros((WIDE, WIDE), jnp.float32)
    grads[...] = jnp.zeros_like(grads)

    def own(k, carry):
        r, c = info[4, k], info[4, 4 + k]
        fr = window(ob, (0,), r, c)
        fi = window(ob, (1,), r, c)
        qr, qi = pr[0], pr[1]
        zr, zi = transform(qr * fr - qi * fi, qr * fi + qi * fr, left, right)
        power = zr * zr + zi * zi
        ratio = amplitude[k] * lax.rsqrt(jnp.maximum(power, amp_floor * amp_floor)) - 1.0
        br, bi = transform(zr * ratio, -(zi * ratio), left, right)
        grads[0] += fr * br - fi * bi
        grads[1] += -(fr * bi) - fi * br
        grads[2] += fr * fr + fi * fi
        deposit(canvas, (0,), r, c, qr * br - qi * bi)
        deposit(canvas, (1,), r, c, -(qr * bi) - qi * br)
        return carry

    lax.fori_loop(0, info[4, 8], own, 0)

    def near(i, carry):
        n, k = i // 4, lax.rem(i, 4)
        r = info[n, k] + TILE * (n // 3) - (TILE - F)
        c = info[n, 4 + k] + TILE * lax.rem(n, 3) - (TILE - F)
        live = k < info[n, 8]
        meets = (r > 0) & (r < F + WIDE) & (c > 0) & (c < F + WIDE)

        @pl.when(live & meets)
        def _():
            deposit(glow, (), r, c, pr[0] * pr[0] + pr[1] * pr[1])

        return carry

    lax.fori_loop(0, 36, near, 0)


def hand_out(canvas, glow, grads, l_out, zl_out, zr_out, up_out, dn_out, g_out):
    l_out[...] = glow[F : F + WIDE, F : F + WIDE]
    zl_out[...] = canvas[:, :, :F]
    zr_out[...] = canvas[:, :, TILE:]
    up_out[...] = canvas[:, :F, F:TILE]
    dn_out[...] = canvas[:, TILE:, F:TILE]
    for p in range(3):
        for h in range(2):
            for t in range(2):
                g_out[pl.ds(4 * p + 2 * t + h, HALF, stride=16), :] = grads[p, h * HALF : (h + 1) * HALF, t * LANES : (t + 1) * LANES]
    for j in range(12, 16):
        g_out[pl.ds(j, HALF, stride=16), :] = jnp.zeros((HALF, LANES), jnp.float32)


def first_kernel(info, amp, left, right, probe, tile, below, beside, corner, *rest):
    (ob, canvas), outs, (pr, glow, grads) = rest[:2], rest[2:8], rest[8:]
    ob[:, :TILE, :TILE] = tile[...]
    ob[:, TILE:, :TILE] = below[...]
    ob[:, :TILE, TILE:] = beside[...]
    ob[:, TILE:, TILE:] = corner[...]
    pr[...] = probe[...]
    visit_frames(info, amp, left, right, ob, pr, canvas, glow, grads)
    hand_out(canvas, glow, grads, *outs)


def gathered_probe(pg, pr):
    for p in range(2):
        for h in range(2):
            for t in range(2):
                pr[p, h * HALF : (h + 1) * HALF, t * LANES : (t + 1) * LANES] = pg[pl.ds(4 * p + 2 * t + h, HALF, stride=8), :]


def refreshed(put, size, o, n, l, zl, zr, cup, cdn, sup, sdn):
    for i in range(size // F):
        for j in range(size // F):
            rows, cols = slice(i * F, (i + 1) * F), slice(j * F, (j + 1) * F)
            scale = 1.0 / (l[rows, cols] + object_damping)
            for p in range(2):
                s = n[p, rows, cols]
                if j == 0:
                    s = s + zl[p, rows, :]
                if j == 2:
                    s = s + zr[p, rows, :]
                if i == 0:
                    s = s + (cdn[p] if j == 1 else sdn[j // 2, p])
                if i == 2:
                    s = s + (cup[p] if j == 1 else sup[j // 2, p])
                put(p, rows, cols, o[p, rows, cols] + s * scale)


def next_kernel(info, amp, left, right, pg, o, n, l, zl, zr, cup, cdn, sup, sdn, *rest):
    (ob, canvas), outs, (pr, glow, grads) = rest[:2], rest[2:8], rest[8:]

    def put(p, rows, cols, value):
        ob[p, rows, cols] = value

    refreshed(put, WIDE, o, n, l, zl, zr, cup, cdn, sup, sdn)
    gathered_probe(pg, pr)
    visit_frames(info, amp, left, right, ob, pr, canvas, glow, grads)
    hand_out(canvas, glow, grads, *outs)


def last_kernel(pg, o, n, l, zl, cdn, sdn, o_out, p_out):
    def put(p, rows, cols, value):
        o_out[p, rows, cols] = value

    refreshed(put, TILE, o, n, l, zl, None, None, cdn, None, sdn)
    gathered_probe(pg, p_out)


def probe_kernel(g, old, new, spread):
    s = jnp.sum(g[...].reshape(HALF, 16, LANES), axis=0)
    value = old[...] + s[:8] / (jnp.concatenate([s[8:12], s[8:12]], 0) + probe_damping)
    new[...] = value
    spread[...] = jnp.broadcast_to(value[None], (HALF, 8, LANES)).reshape(HALF * 8, LANES)


def f32(*shape):
    return jax.ShapeDtypeStruct(shape, jnp.float32)


PARAMS = pltpu.CompilerParams(vmem_limit_bytes=48 << 20)


def call_frames(kernel, *args):
    scratch = [
        pltpu.VMEM((2, F, F), jnp.float32),
        pltpu.VMEM((WIDE + 2 * F, WIDE + 2 * F), jnp.float32),
        pltpu.VMEM((3, F, F), jnp.float32),
    ]
    outs = (
        f32(2, WIDE, WIDE), f32(2, WIDE, WIDE), f32(WIDE, WIDE),
        f32(2, WIDE, F), f32(2, WIDE, F), f32(2, F, F), f32(2, F, F), f32(HALF * 16, LANES),
    )
    return pl.pallas_call(
        kernel,
        out_shape=outs,
        in_specs=[SMEM] + [VMEM] * (len(args) - 1),
        out_specs=[VMEM] * len(outs),
        scratch_shapes=scratch,
        compiler_params=PARAMS,
    )(*args)


def everyone(x):
    return lax.all_to_all(x, ("row", "col"), 0, 0)


def shards(object_field, probe, amplitude, positions, counts):
    me = lax.axis_index(("row", "col"))
    left, right = (jnp.asarray(t) for t in tables())
    amp = amplitude[0, 0]
    mine = jnp.concatenate([positions[0, 0, :, 0], positions[0, 0, :, 1], counts[0], jnp.zeros((7,), jnp.int32)])[None]

    below = passed_along(object_field[:, :F, :], "row", -1)
    beside = passed_along(object_field[:, :, :F], "col", -1)
    info = jnp.concatenate([passed_along(mine, "col", 1), mine, passed_along(mine, "col", -1)], 0)
    info = jnp.concatenate([passed_along(info, "row", 1), info, passed_along(info, "row", -1)], 0)
    corner = passed_along(below[:, :, :F], "col", -1)

    own = lax.dynamic_slice(probe.reshape(2, 2, HALF, 2, LANES), (0, 0, me, 0, 0), (2, 2, 1, 2, LANES))
    own = own[:, :, 0].transpose(0, 2, 1, 3).reshape(8, LANES)

    state = call_frames(first_kernel, info, amp, left, right, probe, object_field, below, beside, corner)
    for sweep in range(PASSES):
        last = sweep == PASSES - 1
        ob, numer, light, to_left, to_right, up, down, grad = state
        grad = grad.reshape(HALF, 16, LANES)
        from_left = passed_along(to_right, "col", 1)
        centre_down = passed_along(down, "row", 1)
        if not last:
            from_right = passed_along(to_left, "col", -1)
            centre_up = passed_along(up, "row", -1)
        to_left, to_right, up, down, grad = lax.optimization_barrier((to_left, to_right, up, down, grad))
        grad = everyone(grad)
        grad, from_left = lax.optimization_barrier((grad, from_left))
        own, spread = pl.pallas_call(
            probe_kernel, out_shape=(f32(8, LANES), f32(HALF * 8, LANES)),
            in_specs=[VMEM] * 2, out_specs=[VMEM] * 2, compiler_params=PARAMS,
        )(grad.reshape(HALF * 16, LANES), own)
        spread = spread.reshape(HALF, 8, LANES)
        if last:
            side_down = (numer[:, TILE:, :F] + from_left[:, TILE:])[None]
            sides = (side_down,)
            got = (passed_along(side_down, "row", 1),)
        else:
            side_up = jnp.stack([numer[:, :F, :F] + from_left[:, :F], numer[:, :F, TILE:] + from_right[:, :F]])
            side_down = jnp.stack([numer[:, TILE:, :F] + from_left[:, TILE:], numer[:, TILE:, TILE:] + from_right[:, TILE:]])
            sides = (side_up, side_down)
            got = (passed_along(side_up, "row", -1), passed_along(side_down, "row", 1))
        sides, spread = lax.optimization_barrier((sides, spread))
        pg = everyone(spread).reshape(HALF * 8, LANES)
        if last:
            return pl.pallas_call(
                last_kernel, out_shape=(f32(2, TILE, TILE), f32(2, F, F)),
                in_specs=[VMEM] * 7, out_specs=[VMEM] * 2, compiler_params=PARAMS,
            )(pg, ob, numer, light, from_left, centre_down, got[0])
        state = call_frames(
            next_kernel, info, amp, left, right, pg, ob, numer, light,
            from_left, from_right, centre_up, centre_down, got[0], got[1],
        )


def solution(mesh):
    return jax.shard_map(
        shards,
        mesh=mesh,
        in_specs=(
            P(None, "row", "col"),
            P(),
            P("row", "col", None, None, None),
            P("row", "col", None, None),
            P("row", "col"),
        ),
        out_specs=(P(None, "row", "col"), P()),
        check_vma=False,
    )
```

```python
import math

import jax
import jax.numpy as jnp
import numpy as np
from jax import lax
from jax.experimental import pallas as pl
from jax.experimental.pallas import tpu as pltpu
from jax.sharding import PartitionSpec as P

PASSES = 3
F = 256
TILE = 512
WIDE = TILE + F
HALF = F // 2
LANES = 128
FRAMES_LIMIT = 18

amp_floor = 0.1
object_damping = 0.5
probe_damping = 1.0

VMEM = pl.BlockSpec(memory_space=pltpu.VMEM)
SMEM = pl.BlockSpec(memory_space=pltpu.SMEM)


def passed_along(block, axis, distance):
    size = lax.axis_size(axis)
    route = [((i - distance) % size, i) for i in range(size)]
    return lax.ppermute(block, axis, route)


def split(x):
    high = x.astype(jnp.bfloat16)
    low = (x - high.astype(jnp.float32)).astype(jnp.bfloat16)
    return high, low


def tables():
    k = np.arange(F)
    angles = (k[:, None] * k[None, :] % F) * (-2.0 * math.pi / F)
    re = np.cos(angles) / math.sqrt(F)
    im = np.sin(angles) / math.sqrt(F)
    left = np.block([[re, -im], [im, re]]).astype(np.float32)
    right = np.block([[re, im], [-im, re]]).astype(np.float32)

    def terms(m):
        high = m.astype(jnp.bfloat16)
        low = (m - high.astype(np.float32)).astype(jnp.bfloat16)
        return high, low

    lh, ll = terms(left)
    rh, rl = terms(right)
    return np.concatenate([lh, lh, ll], 1), np.concatenate([rh, rh, rl], 0)


def stacked(re, im):
    h, l = split(jnp.concatenate([re, im], 0))
    return jnp.concatenate([h, l, h], 0)


def abreast(y):
    h, l = split(jnp.concatenate([y[:F], y[F:]], 1))
    return jnp.concatenate([h, l, h], 1)


def transforms(fields, left, right):
    ys = [jnp.dot(left[...], stacked(re, im), preferred_element_type=jnp.float32) for re, im in fields]
    zs = [jnp.dot(abreast(y), right[...], preferred_element_type=jnp.float32) for y in ys]
    return [(z[:, :F], z[:, F:]) for z in zs]


def window(ref, lead, r, c):
    r0 = pl.multiple_of((r // 8) * 8, 8)
    c0 = pl.multiple_of((c // LANES) * LANES, LANES)
    rs, cs = r - r0, c - c0
    w = ref[lead + (pl.ds(r0, F + 8), pl.ds(c0, F + LANES))]
    lane = lax.broadcasted_iota(jnp.int32, (F + 8, LANES), 1)
    back = lax.rem(LANES - cs, LANES)
    t = [pltpu.roll(w[:, i * LANES : (i + 1) * LANES], back, 1) for i in range(3)]
    w = jnp.concatenate([jnp.where(lane < LANES - cs, t[i], t[i + 1]) for i in range(2)], 1)
    w = pltpu.roll(w.reshape(F // 8 + 1, 8, F), lax.rem(8 - rs, 8), 1)
    sub = lax.broadcasted_iota(jnp.int32, (F // 8, 8, F), 1)
    return jnp.where(sub < 8 - rs, w[:-1], w[1:]).reshape(F, F)


def deposit(ref, lead, r, c, x):
    r0 = pl.multiple_of((r // 8) * 8, 8)
    c0 = pl.multiple_of((c // LANES) * LANES, LANES)
    rs, cs = r - r0, c - c0
    w = pltpu.roll(x.reshape(F // 8, 8, F), rs, 1)
    zero = jnp.zeros((1, 8, F), jnp.float32)
    sub = lax.broadcasted_iota(jnp.int32, (F // 8 + 1, 8, F), 1)
    w = jnp.where(sub >= rs, jnp.concatenate([w, zero], 0), jnp.concatenate([zero, w], 0))
    w = w.reshape(F + 8, F)
    lane = lax.broadcasted_iota(jnp.int32, (F + 8, LANES), 1)
    a = pltpu.roll(w[:, :LANES], cs, 1)
    b = pltpu.roll(w[:, LANES:], cs, 1)
    t = [jnp.where(lane >= cs, a, 0.0), jnp.where(lane >= cs, b, a), jnp.where(lane >= cs, 0.0, b)]
    at = lead + (pl.ds(r0, F + 8), pl.ds(c0, F + LANES))
    ref[at] = ref[at] + jnp.concatenate(t, 1)


def visit_frames(info, amplitude, left, right, ob, pr, canvas, grads):
    canvas[...] = jnp.zeros_like(canvas)
    grads[...] = jnp.zeros_like(grads)
    count = info[4, 8]

    def pair(i, carry):
        slots = (2 * i, 2 * i + 1)
        live = (1.0, (2 * i + 1 < count).astype(jnp.float32))
        at = [(info[4, k], info[4, 4 + k]) for k in slots]
        patches = [[window(ob, (p,), r, c) for p in range(2)] for r, c in at]
        qr, qi = pr[0], pr[1]
        waves = [(qr * fr - qi * fi, qr * fi + qi * fr) for fr, fi in patches]
        turned = []
        for k, w, (zr, zi) in zip(slots, live, transforms(waves, left, right)):
            power = zr * zr + zi * zi
            ratio = (amplitude[k] * lax.rsqrt(jnp.maximum(power, amp_floor * amp_floor)) - 1.0) * w
            turned.append((zr * ratio, -(zi * ratio)))
        for w, (r, c), (fr, fi), (br, bi) in zip(live, at, patches, transforms(turned, left, right)):
            grads[0] += fr * br - fi * bi
            grads[1] -= fr * bi + fi * br
            grads[2] += (fr * fr + fi * fi) * w
            deposit(canvas, (0,), r, c, qr * br - qi * bi)
            deposit(canvas, (1,), r, c, -(qr * bi) - qi * br)
        return carry

    lax.fori_loop(0, (count + 1) // 2, pair, 0)


def hand_out(canvas, pr, zl_out, zr_out, up_out, mid_out, dn_out, p_out):
    zl_out[...] = canvas[:, :, :F]
    zr_out[...] = canvas[:, :, TILE:]
    up_out[:2] = canvas[:, :F, F:TILE]
    mid_out[...] = canvas[:, F:TILE, F:TILE]
    dn_out[:2] = canvas[:, TILE:, F:TILE]
    p_out[...] = pr[...]


def pack_kernel(grads, g_out):
    for p in range(3):
        for h in range(2):
            for t in range(2):
                g_out[pl.ds(4 * p + 2 * t + h, HALF, stride=12), :] = grads[p, h * HALF : (h + 1) * HALF, t * LANES : (t + 1) * LANES]


def first_kernel(info, amp, left, right, probe, tile, below, beside, corner, *rest):
    ob, grads, outs, (pr, canvas) = rest[0], rest[1], rest[2:8], rest[8:]
    ob[:, :TILE, :TILE] = tile[...]
    ob[:, TILE:, :TILE] = below[...]
    ob[:, :TILE, TILE:] = beside[...]
    ob[:, TILE:, TILE:] = corner[...]
    pr[...] = probe[...]
    visit_frames(info, amp, left, right, ob, pr, canvas, grads)
    hand_out(canvas, pr, *outs)


def gathered_probe(pg, pr):
    for p in range(2):
        for h in range(2):
            for t in range(2):
                pr[p, h * HALF : (h + 1) * HALF, t * LANES : (t + 1) * LANES] = pg[pl.ds(4 * p + 2 * t + h, HALF, stride=8), :]


def refreshed(put, size, o, l, zl, zr, up, mid, dn, left_in, right_in, cup, cdn, sup, sdn):
    for i in range(size // F):
        for j in range(size // F):
            rows, cols = slice(i * F, (i + 1) * F), slice(j * F, (j + 1) * F)
            scale = 1.0 / (l[rows, cols] + object_damping)
            for p in range(2):
                if j == 0:
                    s = zl[p, rows, :] + left_in[p, rows, :]
                elif j == 1:
                    s = (up, mid, dn)[i][p]
                else:
                    s = zr[p, rows, :] + right_in[p, rows, :]
                if i == 0:
                    s = s + (cdn[p] if j == 1 else sdn[j // 2, p])
                if i == 2:
                    s = s + (cup[p] if j == 1 else sup[j // 2, p])
                put(p, rows, cols, o[p, rows, cols] + s * scale)


def next_kernel(info, amp, left, right, pg, o, l, zl, zr, up, mid, dn, left_in, right_in, cup, cdn, sup, sdn, *rest):
    ob, grads, outs, (pr, canvas) = rest[0], rest[1], rest[2:8], rest[8:]

    def put(p, rows, cols, value):
        ob[p, rows, cols] = value

    refreshed(put, WIDE, o, l, zl, zr, up, mid, dn, left_in, right_in, cup, cdn, sup, sdn)
    gathered_probe(pg, pr)
    visit_frames(info, amp, left, right, ob, pr, canvas, grads)
    hand_out(canvas, pr, *outs)


def last_kernel(pg, o, l, zl, up, mid, left_in, cdn, sdn, o_out, p_out):
    def put(p, rows, cols, value):
        o_out[p, rows, cols] = value

    refreshed(put, TILE, o, l, zl, None, up, mid, None, left_in, None, None, cdn, None, sdn)
    gathered_probe(pg, p_out)


def glow_kernel(info, pr, out, glow):
    glow[F : F + WIDE, F : F + WIDE] = jnp.zeros((WIDE, WIDE), jnp.float32)

    def near(i, carry):
        n, k = i // 4, lax.rem(i, 4)
        r = info[n, k] + TILE * (n // 3) - (TILE - F)
        c = info[n, 4 + k] + TILE * lax.rem(n, 3) - (TILE - F)
        live = k < info[n, 8]
        meets = (r > 0) & (r < F + WIDE) & (c > 0) & (c < F + WIDE)

        @pl.when(live & meets)
        def _():
            deposit(glow, (), r, c, pr[0] * pr[0] + pr[1] * pr[1])

        return carry

    lax.fori_loop(0, 36, near, 0)
    out[...] = glow[F : F + WIDE, F : F + WIDE]


def middle_kernel(last, g, old, zl, left_in, *rest):
    if last:
        sdn, new, spread = rest
        sdn[0] = zl[:, TILE:] + left_in[:, TILE:]
    else:
        zr, right_in, sup, sdn, new, spread = rest
        sup[0] = zl[:, :F] + left_in[:, :F]
        sup[1] = zr[:, :F] + right_in[:, :F]
        sdn[0] = zl[:, TILE:] + left_in[:, TILE:]
        sdn[1] = zr[:, TILE:] + right_in[:, TILE:]
    s = jnp.sum(g[...].reshape(HALF // 2, 24, LANES), axis=0)
    s = s[:12] + s[12:]
    value = old[...] + s[:8] / (jnp.concatenate([s[8:], s[8:]], 0) + probe_damping)
    new[...] = value
    spread[...] = jnp.broadcast_to(value[None], (HALF, 8, LANES)).reshape(HALF * 8, LANES)


def f32(*shape):
    return jax.ShapeDtypeStruct(shape, jnp.float32)


def call(kernel, args, outs, scratch=(), limit=14, smem=(), cost=None, alias=None):
    return pl.pallas_call(
        kernel,
        out_shape=tuple(outs),
        in_specs=[SMEM if i in smem else VMEM for i in range(len(args))],
        out_specs=tuple(VMEM for _ in outs),
        scratch_shapes=list(scratch),
        compiler_params=pltpu.CompilerParams(vmem_limit_bytes=limit << 20),
        cost_estimate=cost,
        input_output_aliases=alias or {},
    )(*args)


def call_frames(kernel, *args, alias=None):
    scratch = [
        pltpu.VMEM((2, F, F), jnp.float32),
        pltpu.VMEM((2, WIDE, WIDE), jnp.float32),
    ]
    outs = (
        f32(2, WIDE, WIDE), f32(3, F, F), f32(2, WIDE, F), f32(2, WIDE, F),
        f32(3, F, F), f32(2, F, F), f32(3, F, F), f32(2, F, F),
    )
    return call(kernel, args, outs, scratch, limit=FRAMES_LIMIT, smem=(0,), alias=alias)


def glow_of(info, pr):
    return call(
        glow_kernel, (info, pr), (f32(WIDE, WIDE),), [pltpu.VMEM((WIDE + 2 * F, WIDE + 2 * F), jnp.float32)],
        limit=8, smem=(0,), cost=pl.CostEstimate(flops=10 << 20, bytes_accessed=12 << 20, transcendentals=0),
    )[0]


def everyone(x):
    return lax.all_to_all(x, ("row", "col"), 0, 0)


def shards(object_field, probe, amplitude, positions, counts):
    me = lax.axis_index(("row", "col"))
    left, right = (jnp.asarray(t) for t in tables())
    amp = amplitude[0, 0]
    mine = jnp.concatenate([positions[0, 0, :, 0], positions[0, 0, :, 1], counts[0], jnp.zeros((7,), jnp.int32)])[None]

    below = passed_along(object_field[:, :F, :], "row", -1)
    beside = passed_along(object_field[:, :, :F], "col", -1)
    info = jnp.concatenate([passed_along(mine, "col", 1), mine, passed_along(mine, "col", -1)], 0)
    info = jnp.concatenate([passed_along(info, "row", 1), info, passed_along(info, "row", -1)], 0)
    below, info = lax.optimization_barrier((below, info))
    corner = passed_along(below[:, :, :F], "col", -1)
    light = glow_of(info, probe)

    own = lax.dynamic_slice(probe.reshape(2, 2, HALF, 2, LANES), (0, 0, me, 0, 0), (2, 2, 1, 2, LANES))
    own = own[:, :, 0].transpose(0, 2, 1, 3).reshape(8, LANES)
    own, light, corner = lax.optimization_barrier((own, light, corner))

    state = call_frames(first_kernel, info, amp, left, right, probe, object_field, below, beside, corner)
    for sweep in range(PASSES):
        last = sweep == PASSES - 1
        ob, grad, to_left, to_right, up, mid, down, pr = state
        grad = call(pack_kernel, (grad,), (f32(HALF * 12, LANES),))[0].reshape(HALF, 3, 4, LANES)
        from_left = passed_along(to_right, "col", 1)
        centre_down = passed_along(down, "row", 1)
        moved = [from_left, centre_down]
        if not last:
            moved += [passed_along(to_left, "col", -1), passed_along(up, "row", -1)]
        grad, to_left, to_right = lax.optimization_barrier((grad, to_left, to_right))
        grad = everyone(grad)
        grad, moved = lax.optimization_barrier((grad, moved))
        grad = grad.reshape(HALF * 12, LANES)
        tail = (f32(8, LANES), f32(HALF * 8, LANES))
        if last:
            from_left, centre_down = moved
            side_down, own, spread = call(
                lambda *refs: middle_kernel(True, *refs), (grad, own, to_left, from_left), (f32(1, 2, F, F),) + tail,
            )
            sides = (side_down,)
            moved = (passed_along(side_down, "row", 1),)
        else:
            from_left, centre_down, from_right, centre_up = moved
            side_up, side_down, own, spread = call(
                lambda *refs: middle_kernel(False, *refs), (grad, own, to_left, from_left, to_right, from_right),
                (f32(2, 2, F, F), f32(2, 2, F, F)) + tail,
            )
            sides = (side_up, side_down)
            moved = (passed_along(side_up, "row", -1), passed_along(side_down, "row", 1))
        sides, spread = lax.optimization_barrier((sides, spread))
        pg = everyone(spread.reshape(HALF, 2, 4, LANES)).reshape(HALF * 8, LANES)
        pg, pr = lax.optimization_barrier((pg, pr))
        if sweep > 0:
            light = glow_of(info, pr)
        if last:
            return call(
                last_kernel, (pg, ob, light, to_left, up, mid, from_left, centre_down, moved[0]),
                (f32(2, TILE, TILE), f32(2, F, F)),
            )
        state = call_frames(
            next_kernel, info, amp, left, right, pg, ob, light, to_left, to_right, up, mid, down,
            from_left, from_right, centre_up, centre_down, moved[0], moved[1], alias={5: 0},
        )


def solution(mesh):
    return jax.shard_map(
        shards,
        mesh=mesh,
        in_specs=(
            P(None, "row", "col"),
            P(),
            P("row", "col", None, None, None),
            P("row", "col", None, None),
            P("row", "col"),
        ),
        out_specs=(P(None, "row", "col"), P()),
        check_vma=False,
    )
```

```python
import math

import jax
import jax.numpy as jnp
import numpy as np
from jax import lax
from jax.experimental import pallas as pl
from jax.experimental.pallas import tpu as pltpu
from jax.sharding import PartitionSpec as P

PASSES = 3
F = 256
TILE = 512
WIDE = TILE + F
HALF = F // 2
LANES = 128
FRAMES_LIMIT = 24
BESIDE = 6
STRIP = 32

amp_floor = 0.1
object_damping = 0.5
probe_damping = 1.0

VMEM = pl.BlockSpec(memory_space=pltpu.VMEM)
SMEM = pl.BlockSpec(memory_space=pltpu.SMEM)


def passed_along(block, axis, distance):
    size = lax.axis_size(axis)
    route = [((i - distance) % size, i) for i in range(size)]
    return lax.ppermute(block, axis, route)


def split(x):
    high = x.astype(jnp.bfloat16)
    low = (x - high.astype(jnp.float32)).astype(jnp.bfloat16)
    return high, low


def tables():
    k = np.arange(F)
    angles = (k[:, None] * k[None, :] % F) * (-2.0 * math.pi / F)
    re = np.cos(angles) / math.sqrt(F)
    im = np.sin(angles) / math.sqrt(F)
    left = np.block([[re, -im], [im, re]]).astype(np.float32)
    right = np.block([[re, im], [-im, re]]).astype(np.float32)

    def terms(m):
        high = m.astype(jnp.bfloat16)
        low = (m - high.astype(np.float32)).astype(jnp.bfloat16)
        return high, low

    lh, ll = terms(left)
    rh, rl = terms(right)
    return np.concatenate([lh, lh, ll], 1), np.concatenate([rh, rh, rl], 0)


def stacked(re, im):
    h, l = split(jnp.concatenate([re, im], 0))
    return jnp.concatenate([h, l, h], 0)


def abreast(y):
    h, l = split(jnp.concatenate([y[:F], y[F:]], 1))
    return jnp.concatenate([h, l, h], 1)


def transforms(fields, left, right):
    ys = [jnp.dot(left[...], stacked(re, im), preferred_element_type=jnp.float32) for re, im in fields]
    zs = [jnp.dot(abreast(y), right[...], preferred_element_type=jnp.float32) for y in ys]
    return [(z[:, :F], z[:, F:]) for z in zs]


def window(ref, lead, r, c):
    r0 = pl.multiple_of((r // 8) * 8, 8)
    c0 = pl.multiple_of((c // LANES) * LANES, LANES)
    rs, cs = r - r0, c - c0
    w = ref[lead + (pl.ds(r0, F + 8), pl.ds(c0, F + LANES))]
    lane = lax.broadcasted_iota(jnp.int32, (F + 8, LANES), 1)
    back = lax.rem(LANES - cs, LANES)
    t = [pltpu.roll(w[:, i * LANES : (i + 1) * LANES], back, 1) for i in range(3)]
    w = jnp.concatenate([jnp.where(lane < LANES - cs, t[i], t[i + 1]) for i in range(2)], 1)
    w = pltpu.roll(w.reshape(F // 8 + 1, 8, F), lax.rem(8 - rs, 8), 1)
    sub = lax.broadcasted_iota(jnp.int32, (F // 8, 8, F), 1)
    return jnp.where(sub < 8 - rs, w[:-1], w[1:]).reshape(F, F)


def shifted(r, c, x):
    r0 = pl.multiple_of((r // 8) * 8, 8)
    c0 = pl.multiple_of((c // LANES) * LANES, LANES)
    rs, cs = r - r0, c - c0
    w = pltpu.roll(x.reshape(F // 8, 8, F), rs, 1)
    zero = jnp.zeros((1, 8, F), jnp.float32)
    sub = lax.broadcasted_iota(jnp.int32, (F // 8 + 1, 8, F), 1)
    w = jnp.where(sub >= rs, jnp.concatenate([w, zero], 0), jnp.concatenate([zero, w], 0))
    w = w.reshape(F + 8, F)
    lane = lax.broadcasted_iota(jnp.int32, (F + 8, LANES), 1)
    a = pltpu.roll(w[:, :LANES], cs, 1)
    b = pltpu.roll(w[:, LANES:], cs, 1)
    t = [jnp.where(lane >= cs, a, 0.0), jnp.where(lane >= cs, b, a), jnp.where(lane >= cs, 0.0, b)]
    return t, r0, c0


def deposit(ref, r, c, x):
    t, r0, c0 = shifted(r, c, x)
    at = (pl.ds(r0, F + 8), pl.ds(c0, F + LANES))
    ref[at] = ref[at] + jnp.concatenate(t, 1)


def deposit_planes(blocks, r, c, planes):
    moved = [shifted(r, c, x) for x in planes]
    r0, c0 = moved[0][1:]
    for first in range(4):

        @pl.when(c0 == first * LANES)
        def _():
            for i in range(3):
                block, half = divmod(first + i, 2)
                for p in range(2):
                    at = (p, pl.ds(r0, F + 8), slice(half * LANES, (half + 1) * LANES))
                    blocks[block][at] = blocks[block][at] + moved[p][0][i]


def visit_pair(i, mine, amplitude, left, right, ob, pr, blocks, grads, fresh, meanwhile):
    slots = (2 * i, 2 * i + 1)
    live = (1.0, (2 * i + 1 < mine[0, 8]).astype(jnp.float32))
    at = [(mine[0, k], mine[0, 4 + k]) for k in slots]
    patches = [[window(ob, (p,), r, c) for p in range(2)] for r, c in at]
    qr, qi = pr[0], pr[1]
    waves = [(qr * fr - qi * fi, qr * fi + qi * fr) for fr, fi in patches]
    turned = []
    for k, w, (zr, zi) in zip(slots, live, transforms(waves, left, right)):
        power = zr * zr + zi * zi
        ratio = (amplitude[k] * lax.rsqrt(jnp.maximum(power, amp_floor * amp_floor)) - 1.0) * w
        turned.append((zr * ratio, -(zi * ratio)))
    sums = [0.0, 0.0, 0.0]
    updates = []
    meanwhile()
    for w, (fr, fi), (br, bi) in zip(live, patches, transforms(turned, left, right)):
        sums[0] = sums[0] + (fr * br - fi * bi)
        sums[1] = sums[1] - (fr * bi + fi * br)
        sums[2] = sums[2] + (fr * fr + fi * fi) * w
        updates.append((qr * br - qi * bi, -(qr * bi) - qi * br))
    for p in range(3):
        grads[p] = sums[p] if fresh else grads[p] + sums[p]
    for (r, c), update in zip(at, updates):
        deposit_planes(blocks, r, c, update)


def near_frames(infos, listed):
    total = jnp.int32(0)
    for a in range(3):
        for b in range(3):
            for k in range(4):
                r = infos[a][b, k] + (TILE * a - (TILE - F))
                c = infos[a][b, 4 + k] + (TILE * b - (TILE - F))
                use = (k < infos[a][b, 8]) & (r > 0) & (r < F + WIDE) & (c > 0) & (c < F + WIDE)
                listed[0, total] = r
                listed[1, total] = c
                total = total + use.astype(jnp.int32)
    return total


def visit_frames(mine, infos, amplitude, left, right, ob, pr, blocks, glow, grads, listed):
    n = near_frames(infos, listed)
    for block in blocks:
        block[...] = jnp.zeros_like(block)
    glow[F : F + WIDE, F : F + WIDE] = jnp.zeros((WIDE, WIDE), jnp.float32)
    light = pr[0] * pr[0] + pr[1] * pr[1]

    def shine(i):
        used = (i < n).astype(jnp.float32)
        at = jnp.where(i < n, i, 0)
        deposit(glow, listed[0, at], listed[1, at], light * used)

    def shine_some(start):
        for i in range(start, start + BESIDE):
            shine(i)

    visit_pair(0, mine, amplitude, left, right, ob, pr, blocks, grads, True, lambda: shine_some(0))

    @pl.when(mine[0, 8] > 2)
    def _():
        visit_pair(1, mine, amplitude, left, right, ob, pr, blocks, grads, False, lambda: shine_some(BESIDE))

    done = jnp.where(mine[0, 8] > 2, 2 * BESIDE, BESIDE)

    def more(i, carry):
        shine(i)
        return carry

    lax.fori_loop(done, n, more, 0)


def hand_out(middle, grads, up_out, mid_out, dn_out, g_out):
    up_out[:2] = middle[:, :F]
    mid_out[...] = middle[:, F:TILE]
    dn_out[:2] = middle[:, TILE:]
    for p in range(3):
        for h in range(2):
            for t in range(2):
                g_out[pl.ds(4 * p + 2 * t + h, HALF, stride=12), :] = grads[p, h * HALF : (h + 1) * HALF, t * LANES : (t + 1) * LANES]


def start_kernel(tile, probe, ob, pr, own):
    ob[:, :TILE, :TILE] = tile[...]
    pr[...] = probe[...]
    me = lax.axis_index("row") * lax.axis_size("col") + lax.axis_index("col")
    picked = lax.broadcasted_iota(jnp.int32, (HALF, LANES), 0) == me
    rows = []
    for p in range(2):
        for t in range(2):
            for h in range(2):
                rows.append(jnp.sum(jnp.where(picked, probe[p, h * HALF : (h + 1) * HALF, t * LANES : (t + 1) * LANES], 0.0), axis=0, keepdims=True))
    own[...] = jnp.concatenate(rows, 0)


def first_kernel(mine, ia, ib, ic, amp, left, right, pr, tile, below, below_right, beside, corner, *rest):
    ob, light, zl, zr, outs, (unused, middle, grads, listed, glow) = rest[0], rest[1], rest[2], rest[3], rest[4:8], rest[8:]
    ob[:, TILE:, :F] = below[...]
    ob[:, TILE:, F:TILE] = below_right[...]
    ob[:, :TILE, TILE:] = beside[...]
    ob[:, TILE:, TILE:] = corner[...]
    visit_frames(mine, (ia, ib, ic), amp, left, right, ob, pr, (zl, middle, zr), glow, grads, listed)
    light[...] = glow[F : F + WIDE, F : F + WIDE]
    hand_out(middle, grads, *outs)


def gathered_probe(pg, pr):
    for p in range(2):
        for h in range(2):
            for t in range(2):
                pr[p, h * HALF : (h + 1) * HALF, t * LANES : (t + 1) * LANES] = pg[pl.ds(4 * p + 2 * t + h, HALF, stride=8), :]


def refreshed(put, size, o, l, zl, zr, up, mid, dn, left_in, right_in, cup, cdn, sup, sdn):
    for i in range(size // F):
        for j in range(size // F):
            for at in range(0, F, STRIP):
                here = slice(at, at + STRIP)
                rows, cols = slice(i * F + at, i * F + at + STRIP), slice(j * F, (j + 1) * F)
                scale = 1.0 / (l[rows, cols] + object_damping)
                for p in range(2):
                    if j == 0:
                        s = zl[p, rows, :] + left_in[p, rows, :]
                    elif j == 1:
                        s = (up, mid, dn)[i][p, here, :]
                    else:
                        s = zr[p, rows, :] + right_in[p, rows, :]
                    if i == 0:
                        s = s + (cdn[p, here, :] if j == 1 else sdn[j // 2, p, here, :])
                    if i == 2:
                        s = s + (cup[p, here, :] if j == 1 else sup[j // 2, p, here, :])
                    put(p, rows, cols, o[p, rows, cols] + s * scale)


def next_kernel(mine, ia, ib, ic, amp, left, right, pg, o, l, zl, zr, up, mid, dn, left_in, right_in, cup, cdn, sup, sdn, *rest):
    ob, light, zl_out, zr_out, outs, (pr, middle, grads, listed, glow) = rest[0], rest[1], rest[2], rest[3], rest[4:8], rest[8:]

    def put(p, rows, cols, value):
        ob[p, rows, cols] = value

    refreshed(put, WIDE, o, l, zl, zr, up, mid, dn, left_in, right_in, cup, cdn, sup, sdn)
    gathered_probe(pg, pr)
    visit_frames(mine, (ia, ib, ic), amp, left, right, ob, pr, (zl_out, middle, zr_out), glow, grads, listed)
    light[...] = glow[F : F + WIDE, F : F + WIDE]
    hand_out(middle, grads, *outs)


def last_kernel(pg, o, l, zl, up, mid, left_in, cdn, sdn, o_out, p_out):
    def put(p, rows, cols, value):
        o_out[p, rows, cols] = value

    refreshed(put, TILE, o, l, zl, None, up, mid, None, left_in, None, None, cdn, None, sdn)
    gathered_probe(pg, p_out)


def middle_kernel(last, g, old, zl, left_in, *rest):
    if last:
        sdn, new, spread = rest
        sdn[0] = zl[:, TILE:] + left_in[:, TILE:]
    else:
        zr, right_in, sup, sdn, new, spread = rest
        sup[0] = zl[:, :F] + left_in[:, :F]
        sup[1] = zr[:, :F] + right_in[:, :F]
        sdn[0] = zl[:, TILE:] + left_in[:, TILE:]
        sdn[1] = zr[:, TILE:] + right_in[:, TILE:]
    s = jnp.sum(g[...].reshape(HALF // 2, 24, LANES), axis=0)
    s = s[:12] + s[12:]
    value = old[...] + s[:8] / (jnp.concatenate([s[8:], s[8:]], 0) + probe_damping)
    new[...] = value
    spread[...] = jnp.broadcast_to(value[None], (HALF, 8, LANES)).reshape(HALF * 8, LANES)


def f32(*shape):
    return jax.ShapeDtypeStruct(shape, jnp.float32)


def call(kernel, args, outs, scratch=(), limit=14, smem=(), cost=None, alias=None):
    return pl.pallas_call(
        kernel,
        out_shape=tuple(outs),
        in_specs=[SMEM if i in smem else VMEM for i in range(len(args))],
        out_specs=tuple(VMEM for _ in outs),
        scratch_shapes=list(scratch),
        compiler_params=pltpu.CompilerParams(vmem_limit_bytes=limit << 20),
        cost_estimate=cost,
        input_output_aliases=alias or {},
    )(*args)


def call_frames(kernel, *args, alias=None):
    scratch = [
        pltpu.VMEM((2, F, F), jnp.float32),
        pltpu.VMEM((2, WIDE, F), jnp.float32),
        pltpu.VMEM((3, F, F), jnp.float32),
        pltpu.SMEM((2, 40), jnp.int32),
        pltpu.VMEM((WIDE + 2 * F, WIDE + 2 * F), jnp.float32),
    ]
    outs = (
        f32(2, WIDE, WIDE), f32(WIDE, WIDE), f32(2, WIDE, F), f32(2, WIDE, F),
        f32(3, F, F), f32(2, F, F), f32(3, F, F), f32(HALF * 12, LANES),
    )
    return call(kernel, args, outs, scratch, limit=FRAMES_LIMIT, smem=(0, 1, 2, 3), alias=alias)


def everyone(x):
    return lax.all_to_all(x, ("row", "col"), 0, 0)


def shards(object_field, probe, amplitude, positions, counts):
    left, right = (jnp.asarray(t) for t in tables())
    amp = amplitude[0, 0]
    mine = jnp.concatenate([positions[0, 0, :, 0], positions[0, 0, :, 1], counts[0], jnp.zeros((7,), jnp.int32)])[None]

    below = passed_along(object_field[:, :F, :F], "row", -1)
    beside = passed_along(object_field[:, :, :F], "col", -1)
    below_right = passed_along(object_field[:, :F, F:], "row", -1)
    info = jnp.concatenate([passed_along(mine, "col", 1), mine, passed_along(mine, "col", -1)], 0)
    below, info = lax.optimization_barrier((below, info))
    infos = (passed_along(info, "row", 1), info, passed_along(info, "row", -1))
    corner = passed_along(below, "col", -1)
    wide, probe, own = call(start_kernel, (object_field, probe), (f32(2, WIDE, WIDE), f32(2, F, F), f32(8, LANES)))

    state = call_frames(
        first_kernel, mine, *infos, amp, left, right, probe, wide, below, below_right, beside, corner, alias={8: 0},
    )
    for sweep in range(PASSES):
        last = sweep == PASSES - 1
        ob, light, to_left, to_right, up, mid, down, grad = state
        grad = grad.reshape(HALF, 3, 4, LANES)
        from_left = passed_along(to_right, "col", 1)
        centre_down = passed_along(down, "row", 1)
        moved = [from_left, centre_down]
        if not last:
            moved += [passed_along(to_left, "col", -1), passed_along(up, "row", -1)]
        grad, to_left, to_right = lax.optimization_barrier((grad, to_left, to_right))
        grad = everyone(grad)
        grad, moved = lax.optimization_barrier((grad, moved))
        grad = grad.reshape(HALF * 12, LANES)
        tail = (f32(8, LANES), f32(HALF * 8, LANES))
        if last:
            from_left, centre_down = moved
            side_down, own, spread = call(
                lambda *refs: middle_kernel(True, *refs), (grad, own, to_left, from_left), (f32(1, 2, F, F),) + tail,
            )
            sides = (side_down,)
            moved = (passed_along(side_down, "row", 1),)
        else:
            from_left, centre_down, from_right, centre_up = moved
            side_up, side_down, own, spread = call(
                lambda *refs: middle_kernel(False, *refs), (grad, own, to_left, from_left, to_right, from_right),
                (f32(2, 2, F, F), f32(2, 2, F, F)) + tail,
            )
            sides = (side_up, side_down)
            moved = (passed_along(side_up, "row", -1), passed_along(side_down, "row", 1))
        sides, spread = lax.optimization_barrier((sides, spread))
        pg = everyone(spread.reshape(HALF, 2, 4, LANES)).reshape(HALF * 8, LANES)
        if last:
            return call(
                last_kernel, (pg, ob, light, to_left, up, mid, from_left, centre_down, moved[0]),
                (f32(2, TILE, TILE), f32(2, F, F)),
            )
        state = call_frames(
            next_kernel, mine, *infos, amp, left, right, pg, ob, light, to_left, to_right, up, mid, down,
            from_left, from_right, centre_up, centre_down, moved[0], moved[1], alias={8: 0},
        )


def solution(mesh):
    return jax.shard_map(
        shards,
        mesh=mesh,
        in_specs=(
            P(None, "row", "col"),
            P(),
            P("row", "col", None, None, None),
            P("row", "col", None, None),
            P("row", "col"),
        ),
        out_specs=(P(None, "row", "col"), P()),
        check_vma=False,
    )
```

```python
import math

import jax
import jax.numpy as jnp
import numpy as np
from jax import lax
from jax.experimental import pallas as pl
from jax.experimental.pallas import tpu as pltpu
from jax.sharding import PartitionSpec as P

PASSES = 3
F = 256
TILE = 512
WIDE = TILE + F
HALF = F // 2
LANES = 128
FRAMES_LIMIT = 20
BESIDE = 6
STRIP = 32

amp_floor = 0.1
object_damping = 0.5
probe_damping = 1.0

VMEM = pl.BlockSpec(memory_space=pltpu.VMEM)
SMEM = pl.BlockSpec(memory_space=pltpu.SMEM)


def passed_along(block, axis, distance):
    size = lax.axis_size(axis)
    route = [((i - distance) % size, i) for i in range(size)]
    return lax.ppermute(block, axis, route)


def split(x):
    high = x.astype(jnp.bfloat16)
    low = (x - high.astype(jnp.float32)).astype(jnp.bfloat16)
    return high, low


def tables():
    k = np.arange(F)
    angles = (k[:, None] * k[None, :] % F) * (-2.0 * math.pi / F)
    re = np.cos(angles) / math.sqrt(F)
    im = np.sin(angles) / math.sqrt(F)
    left = np.block([[re, -im], [im, re]]).astype(np.float32)
    right = np.block([[re, im], [-im, re]]).astype(np.float32)

    def terms(m):
        high = m.astype(jnp.bfloat16)
        low = (m - high.astype(np.float32)).astype(jnp.bfloat16)
        return high, low

    lh, ll = terms(left)
    rh, rl = terms(right)
    return np.concatenate([lh, lh, ll], 1), np.concatenate([rh, rh, rl], 0)


def stacked(re, im):
    h, l = split(jnp.concatenate([re, im], 0))
    return jnp.concatenate([h, l, h], 0)


def abreast(y):
    h, l = split(jnp.concatenate([y[:F], y[F:]], 1))
    return jnp.concatenate([h, l, h], 1)


def transforms(fields, left, right):
    ys = [jnp.dot(left[...], stacked(re, im), preferred_element_type=jnp.float32) for re, im in fields]
    zs = [jnp.dot(abreast(y), right[...], preferred_element_type=jnp.float32) for y in ys]
    return [(z[:, :F], z[:, F:]) for z in zs]


def window(ref, lead, r, c):
    r0 = pl.multiple_of((r // 8) * 8, 8)
    c0 = pl.multiple_of((c // LANES) * LANES, LANES)
    rs, cs = r - r0, c - c0
    w = ref[lead + (pl.ds(r0, F + 8), pl.ds(c0, F + LANES))]
    lane = lax.broadcasted_iota(jnp.int32, (F + 8, LANES), 1)
    back = lax.rem(LANES - cs, LANES)
    t = [pltpu.roll(w[:, i * LANES : (i + 1) * LANES], back, 1) for i in range(3)]
    w = jnp.concatenate([jnp.where(lane < LANES - cs, t[i], t[i + 1]) for i in range(2)], 1)
    w = pltpu.roll(w.reshape(F // 8 + 1, 8, F), lax.rem(8 - rs, 8), 1)
    sub = lax.broadcasted_iota(jnp.int32, (F // 8, 8, F), 1)
    return jnp.where(sub < 8 - rs, w[:-1], w[1:]).reshape(F, F)


def shifted(r, c, x):
    r0 = pl.multiple_of((r // 8) * 8, 8)
    c0 = pl.multiple_of((c // LANES) * LANES, LANES)
    rs, cs = r - r0, c - c0
    w = pltpu.roll(x.reshape(F // 8, 8, F), rs, 1)
    zero = jnp.zeros((1, 8, F), jnp.float32)
    sub = lax.broadcasted_iota(jnp.int32, (F // 8 + 1, 8, F), 1)
    w = jnp.where(sub >= rs, jnp.concatenate([w, zero], 0), jnp.concatenate([zero, w], 0))
    w = w.reshape(F + 8, F)
    lane = lax.broadcasted_iota(jnp.int32, (F + 8, LANES), 1)
    a = pltpu.roll(w[:, :LANES], cs, 1)
    b = pltpu.roll(w[:, LANES:], cs, 1)
    t = [jnp.where(lane >= cs, a, 0.0), jnp.where(lane >= cs, b, a), jnp.where(lane >= cs, 0.0, b)]
    return t, r0, c0


def deposit(ref, r, c, x):
    t, r0, c0 = shifted(r, c, x)
    at = (pl.ds(r0, F + 8), pl.ds(c0, F + LANES))
    ref[at] = ref[at] + jnp.concatenate(t, 1)


def deposit_planes(blocks, r, c, planes):
    moved = [shifted(r, c, x) for x in planes]
    r0, c0 = moved[0][1:]
    for first in range(4):

        @pl.when(c0 == first * LANES)
        def _():
            for i in range(3):
                block, half = divmod(first + i, 2)
                for p in range(2):
                    at = (p, pl.ds(r0, F + 8), slice(half * LANES, (half + 1) * LANES))
                    blocks[block][at] = blocks[block][at] + moved[p][0][i]


def visit_pair(i, mine, amplitude, left, right, ob, pr, blocks, grads, fresh, meanwhile):
    slots = (2 * i, 2 * i + 1)
    live = (1.0, (2 * i + 1 < mine[0, 8]).astype(jnp.float32))
    at = [(mine[0, k], mine[0, 4 + k]) for k in slots]
    patches = [[window(ob, (p,), r, c) for p in range(2)] for r, c in at]
    qr, qi = pr[0], pr[1]
    waves = [(qr * fr - qi * fi, qr * fi + qi * fr) for fr, fi in patches]
    turned = []
    for k, w, (zr, zi) in zip(slots, live, transforms(waves, left, right)):
        power = zr * zr + zi * zi
        ratio = (amplitude[k] * lax.rsqrt(jnp.maximum(power, amp_floor * amp_floor)) - 1.0) * w
        turned.append((zr * ratio, -(zi * ratio)))
    sums = [0.0, 0.0, 0.0]
    updates = []
    meanwhile()
    for w, (fr, fi), (br, bi) in zip(live, patches, transforms(turned, left, right)):
        sums[0] = sums[0] + (fr * br - fi * bi)
        sums[1] = sums[1] - (fr * bi + fi * br)
        sums[2] = sums[2] + (fr * fr + fi * fi) * w
        updates.append((qr * br - qi * bi, -(qr * bi) - qi * br))
    for p in range(3):
        grads[p] = sums[p] if fresh else grads[p] + sums[p]
    for (r, c), update in zip(at, updates):
        deposit_planes(blocks, r, c, update)


def near_frames(infos, listed):
    total = jnp.int32(0)
    for a in range(3):
        for b in range(3):
            for k in range(4):
                r = infos[a][b, k] + (TILE * a - (TILE - F))
                c = infos[a][b, 4 + k] + (TILE * b - (TILE - F))
                use = (k < infos[a][b, 8]) & (r > 0) & (r < F + WIDE) & (c > 0) & (c < F + WIDE)
                listed[0, total] = r
                listed[1, total] = c
                total = total + use.astype(jnp.int32)
    return total


def visit_frames(mine, infos, amplitude, left, right, ob, pr, blocks, glow, grads, listed):
    n = near_frames(infos, listed)
    for block in blocks:
        block[...] = jnp.zeros_like(block)
    glow[F : F + WIDE, F : F + WIDE] = jnp.zeros((WIDE, WIDE), jnp.float32)
    light = pr[0] * pr[0] + pr[1] * pr[1]

    def shine(i):
        used = (i < n).astype(jnp.float32)
        at = jnp.where(i < n, i, 0)
        deposit(glow, listed[0, at], listed[1, at], light * used)

    def shine_some(start):
        for i in range(start, start + BESIDE):
            shine(i)

    visit_pair(0, mine, amplitude, left, right, ob, pr, blocks, grads, True, lambda: shine_some(0))

    @pl.when(mine[0, 8] > 2)
    def _():
        visit_pair(1, mine, amplitude, left, right, ob, pr, blocks, grads, False, lambda: shine_some(BESIDE))

    done = jnp.where(mine[0, 8] > 2, 2 * BESIDE, BESIDE)

    def more(i, carry):
        shine(i)
        return carry

    lax.fori_loop(done, n, more, 0)


def hand_out(middle, grads, up_out, mid_out, dn_out, g_out):
    up_out[:2] = middle[:, :F]
    mid_out[...] = middle[:, F:TILE]
    dn_out[:2] = middle[:, TILE:]
    for p in range(3):
        for h in range(2):
            for t in range(2):
                g_out[pl.ds(4 * p + 2 * t + h, HALF, stride=12), :] = grads[p, h * HALF : (h + 1) * HALF, t * LANES : (t + 1) * LANES]


def start_kernel(tile, probe, ob, pr, own):
    ob[:, :TILE, :TILE] = tile[...]
    pr[...] = probe[...]
    me = lax.axis_index("row") * lax.axis_size("col") + lax.axis_index("col")
    picked = lax.broadcasted_iota(jnp.int32, (HALF, LANES), 0) == me
    rows = []
    for p in range(2):
        for t in range(2):
            for h in range(2):
                rows.append(jnp.sum(jnp.where(picked, probe[p, h * HALF : (h + 1) * HALF, t * LANES : (t + 1) * LANES], 0.0), axis=0, keepdims=True))
    own[...] = jnp.concatenate(rows, 0)


def first_kernel(mine, ia, ib, ic, amp, left, right, pr, tile, below, below_right, beside, corner, *rest):
    ob, light, zl, zr, outs, (unused, middle, grads, listed, glow) = rest[0], rest[1], rest[2], rest[3], rest[4:8], rest[8:]
    ob[:, TILE:, :F] = below[...]
    ob[:, TILE:, F:TILE] = below_right[...]
    ob[:, :TILE, TILE:] = beside[...]
    ob[:, TILE:, TILE:] = corner[...]
    visit_frames(mine, (ia, ib, ic), amp, left, right, ob, pr, (zl, middle, zr), glow, grads, listed)
    light[...] = glow[F : F + WIDE, F : F + WIDE]
    hand_out(middle, grads, *outs)


def gathered_probe(pg, pr):
    for p in range(2):
        for h in range(2):
            for t in range(2):
                pr[p, h * HALF : (h + 1) * HALF, t * LANES : (t + 1) * LANES] = pg[pl.ds(4 * p + 2 * t + h, HALF, stride=8), :]


def refreshed(put, size, o, l, zl, zr, up, mid, dn, left_in, right_in, cup, cdn, sup, sdn):
    for i in range(size // F):
        for j in range(size // F):
            for at in range(0, F, STRIP):
                here = slice(at, at + STRIP)
                rows, cols = slice(i * F + at, i * F + at + STRIP), slice(j * F, (j + 1) * F)
                scale = 1.0 / (l[rows, cols] + object_damping)
                for p in range(2):
                    if j == 0:
                        s = zl[p, rows, :] + left_in[p, rows, :]
                    elif j == 1:
                        s = (up, mid, dn)[i][p, here, :]
                    else:
                        s = zr[p, rows, :] + right_in[p, rows, :]
                    if i == 0:
                        s = s + (cdn[p, here, :] if j == 1 else sdn[j // 2, p, here, :])
                    if i == 2:
                        s = s + (cup[p, here, :] if j == 1 else sup[j // 2, p, here, :])
                    put(p, rows, cols, o[p, rows, cols] + s * scale)


def next_kernel(mine, ia, ib, ic, amp, left, right, pg, o, l, zl, zr, up, mid, dn, left_in, right_in, cup, cdn, sup, sdn, *rest):
    ob, light, zl_out, zr_out, outs, (pr, middle, grads, listed, glow) = rest[0], rest[1], rest[2], rest[3], rest[4:8], rest[8:]

    def put(p, rows, cols, value):
        ob[p, rows, cols] = value

    refreshed(put, WIDE, o, l, zl, zr, up, mid, dn, left_in, right_in, cup, cdn, sup, sdn)
    gathered_probe(pg, pr)
    visit_frames(mine, (ia, ib, ic), amp, left, right, ob, pr, (zl_out, middle, zr_out), glow, grads, listed)
    light[...] = glow[F : F + WIDE, F : F + WIDE]
    hand_out(middle, grads, *outs)


def last_kernel(pg, o, l, zl, up, mid, left_in, cdn, sdn, o_out, p_out):
    def put(p, rows, cols, value):
        o_out[p, rows, cols] = value

    refreshed(put, TILE, o, l, zl, None, up, mid, None, left_in, None, None, cdn, None, sdn)
    gathered_probe(pg, p_out)


def middle_kernel(last, g, old, zl, left_in, *rest):
    if last:
        sdn, new, spread = rest
        sdn[0] = zl[:, TILE:] + left_in[:, TILE:]
    else:
        zr, right_in, sup, sdn, new, spread = rest
        sup[0] = zl[:, :F] + left_in[:, :F]
        sup[1] = zr[:, :F] + right_in[:, :F]
        sdn[0] = zl[:, TILE:] + left_in[:, TILE:]
        sdn[1] = zr[:, TILE:] + right_in[:, TILE:]
    s = jnp.sum(g[...].reshape(HALF // 2, 24, LANES), axis=0)
    s = s[:12] + s[12:]
    value = old[...] + s[:8] / (jnp.concatenate([s[8:], s[8:]], 0) + probe_damping)
    new[...] = value
    spread[...] = jnp.broadcast_to(value[None], (HALF, 8, LANES)).reshape(HALF * 8, LANES)


def f32(*shape):
    return jax.ShapeDtypeStruct(shape, jnp.float32)


def call(kernel, args, outs, scratch=(), limit=14, smem=(), cost=None, alias=None):
    return pl.pallas_call(
        kernel,
        out_shape=tuple(outs),
        in_specs=[SMEM if i in smem else VMEM for i in range(len(args))],
        out_specs=tuple(VMEM for _ in outs),
        scratch_shapes=list(scratch),
        compiler_params=pltpu.CompilerParams(vmem_limit_bytes=limit << 20),
        cost_estimate=cost,
        input_output_aliases=alias or {},
    )(*args)


def call_frames(kernel, *args, alias=None):
    scratch = [
        pltpu.VMEM((2, F, F), jnp.float32),
        pltpu.VMEM((2, WIDE, F), jnp.float32),
        pltpu.VMEM((3, F, F), jnp.float32),
        pltpu.SMEM((2, 40), jnp.int32),
        pltpu.VMEM((WIDE + 2 * F, WIDE + 2 * F), jnp.float32),
    ]
    outs = (
        f32(2, WIDE, WIDE), f32(WIDE, WIDE), f32(2, WIDE, F), f32(2, WIDE, F),
        f32(3, F, F), f32(2, F, F), f32(3, F, F), f32(HALF * 12, LANES),
    )
    return call(kernel, args, outs, scratch, limit=FRAMES_LIMIT, smem=(0, 1, 2, 3), alias=alias)


def everyone(x):
    return lax.all_to_all(x, ("row", "col"), 0, 0)


def shards(object_field, probe, amplitude, positions, counts):
    left, right = (jnp.asarray(t) for t in tables())
    amp = amplitude[0, 0]
    mine = jnp.concatenate([positions[0, 0, :, 0], positions[0, 0, :, 1], counts[0], jnp.zeros((7,), jnp.int32)])[None]

    below = passed_along(object_field[:, :F, :F], "row", -1)
    beside = passed_along(object_field[:, :, :F], "col", -1)
    below_right = passed_along(object_field[:, :F, F:], "row", -1)
    info = jnp.concatenate([passed_along(mine, "col", 1), mine, passed_along(mine, "col", -1)], 0)
    below, info = lax.optimization_barrier((below, info))
    infos = (passed_along(info, "row", 1), info, passed_along(info, "row", -1))
    corner = passed_along(below, "col", -1)
    wide, probe, own = call(start_kernel, (object_field, probe), (f32(2, WIDE, WIDE), f32(2, F, F), f32(8, LANES)))

    state = call_frames(
        first_kernel, mine, *infos, amp, left, right, probe, wide, below, below_right, beside, corner, alias={8: 0},
    )
    for sweep in range(PASSES):
        last = sweep == PASSES - 1
        ob, light, to_left, to_right, up, mid, down, grad = state
        grad = grad.reshape(HALF, 3, 4, LANES)
        from_left = passed_along(to_right, "col", 1)
        centre_down = passed_along(down, "row", 1)
        moved = [from_left, centre_down]
        if not last:
            moved += [passed_along(to_left, "col", -1), passed_along(up, "row", -1)]
        grad, to_left, to_right = lax.optimization_barrier((grad, to_left, to_right))
        grad = everyone(grad)
        grad, moved = lax.optimization_barrier((grad, moved))
        grad = grad.reshape(HALF * 12, LANES)
        tail = (f32(8, LANES), f32(HALF * 8, LANES))
        if last:
            from_left, centre_down = moved
            side_down, own, spread = call(
                lambda *refs: middle_kernel(True, *refs), (grad, own, to_left, from_left), (f32(1, 2, F, F),) + tail,
            )
            sides = (side_down,)
            moved = (passed_along(side_down, "row", 1),)
        else:
            from_left, centre_down, from_right, centre_up = moved
            side_up, side_down, own, spread = call(
                lambda *refs: middle_kernel(False, *refs), (grad, own, to_left, from_left, to_right, from_right),
                (f32(2, 2, F, F), f32(2, 2, F, F)) + tail,
            )
            sides = (side_up, side_down)
            moved = (passed_along(side_up, "row", -1), passed_along(side_down, "row", 1))
        sides, spread = lax.optimization_barrier((sides, spread))
        pg = everyone(spread.reshape(HALF, 2, 4, LANES)).reshape(HALF * 8, LANES)
        if last:
            return call(
                last_kernel, (pg, ob, light, to_left, up, mid, from_left, centre_down, moved[0]),
                (f32(2, TILE, TILE), f32(2, F, F)),
            )
        state = call_frames(
            next_kernel, mine, *infos, amp, left, right, pg, ob, light, to_left, to_right, up, mid, down,
            from_left, from_right, centre_up, centre_down, moved[0], moved[1], alias={8: 0},
        )


def solution(mesh):
    return jax.shard_map(
        shards,
        mesh=mesh,
        in_specs=(
            P(None, "row", "col"),
            P(),
            P("row", "col", None, None, None),
            P("row", "col", None, None),
            P("row", "col"),
        ),
        out_specs=(P(None, "row", "col"), P()),
        check_vma=False,
    )
```

```python
import math

import jax
import jax.numpy as jnp
import numpy as np
from jax import lax
from jax.experimental import pallas as pl
from jax.experimental.pallas import tpu as pltpu
from jax.sharding import PartitionSpec as P

PASSES = 3
F = 256
TILE = 512
WIDE = TILE + F
HALF = F // 2
LANES = 128
FRAMES_LIMIT = 22
BESIDE = 6
STRIP = 32

amp_floor = 0.1
object_damping = 0.5
probe_damping = 1.0

VMEM = pl.BlockSpec(memory_space=pltpu.VMEM)
SMEM = pl.BlockSpec(memory_space=pltpu.SMEM)


def passed_along(block, axis, distance):
    size = lax.axis_size(axis)
    route = [((i - distance) % size, i) for i in range(size)]
    return lax.ppermute(block, axis, route)


def split(x):
    high = x.astype(jnp.bfloat16)
    low = (x - high.astype(jnp.float32)).astype(jnp.bfloat16)
    return high, low


def tables():
    k = np.arange(F)
    angles = (k[:, None] * k[None, :] % F) * (-2.0 * math.pi / F)
    re = np.cos(angles) / math.sqrt(F)
    im = np.sin(angles) / math.sqrt(F)
    left = np.block([[re, -im], [im, re]]).astype(np.float32)
    right = np.block([[re, im], [-im, re]]).astype(np.float32)

    def terms(m):
        high = m.astype(jnp.bfloat16)
        low = (m - high.astype(np.float32)).astype(jnp.bfloat16)
        return high, low

    lh, ll = terms(left)
    rh, rl = terms(right)
    return np.concatenate([lh, lh, ll], 1), np.concatenate([rh, rh, rl], 0)


def stacked(re, im):
    h, l = split(jnp.concatenate([re, im], 0))
    return jnp.concatenate([h, l, h], 0)


def abreast(y):
    h, l = split(jnp.concatenate([y[:F], y[F:]], 1))
    return jnp.concatenate([h, l, h], 1)


def transforms(fields, left, right):
    ys = [jnp.dot(left[...], stacked(re, im), preferred_element_type=jnp.float32) for re, im in fields]
    zs = [jnp.dot(abreast(y), right[...], preferred_element_type=jnp.float32) for y in ys]
    return [(z[:, :F], z[:, F:]) for z in zs]


def window(ref, lead, r, c):
    r0 = pl.multiple_of((r // 8) * 8, 8)
    c0 = pl.multiple_of((c // LANES) * LANES, LANES)
    rs, cs = r - r0, c - c0
    w = ref[lead + (pl.ds(r0, F + 8), pl.ds(c0, F + LANES))]
    lane = lax.broadcasted_iota(jnp.int32, (F + 8, LANES), 1)
    back = lax.rem(LANES - cs, LANES)
    t = [pltpu.roll(w[:, i * LANES : (i + 1) * LANES], back, 1) for i in range(3)]
    w = jnp.concatenate([jnp.where(lane < LANES - cs, t[i], t[i + 1]) for i in range(2)], 1)
    w = pltpu.roll(w.reshape(F // 8 + 1, 8, F), lax.rem(8 - rs, 8), 1)
    sub = lax.broadcasted_iota(jnp.int32, (F // 8, 8, F), 1)
    return jnp.where(sub < 8 - rs, w[:-1], w[1:]).reshape(F, F)


def deposit(ref, lead, r, c, x):
    r0 = pl.multiple_of((r // 8) * 8, 8)
    c0 = pl.multiple_of((c // LANES) * LANES, LANES)
    rs, cs = r - r0, c - c0
    w = pltpu.roll(x.reshape(F // 8, 8, F), rs, 1)
    zero = jnp.zeros((1, 8, F), jnp.float32)
    sub = lax.broadcasted_iota(jnp.int32, (F // 8 + 1, 8, F), 1)
    w = jnp.where(sub >= rs, jnp.concatenate([w, zero], 0), jnp.concatenate([zero, w], 0))
    w = w.reshape(F + 8, F)
    lane = lax.broadcasted_iota(jnp.int32, (F + 8, LANES), 1)
    a = pltpu.roll(w[:, :LANES], cs, 1)
    b = pltpu.roll(w[:, LANES:], cs, 1)
    t = [jnp.where(lane >= cs, a, 0.0), jnp.where(lane >= cs, b, a), jnp.where(lane >= cs, 0.0, b)]
    at = lead + (pl.ds(r0, F + 8), pl.ds(c0, F + LANES))
    ref[at] = ref[at] + jnp.concatenate(t, 1)


def visit_pair(i, mine, amplitude, left, right, ob, pr, canvas, grads):
    slots = (2 * i, 2 * i + 1)
    live = (1.0, (2 * i + 1 < mine[0, 8]).astype(jnp.float32))
    at = [(mine[0, k], mine[0, 4 + k]) for k in slots]
    patches = [[window(ob, (p,), r, c) for p in range(2)] for r, c in at]
    qr, qi = pr[0], pr[1]
    waves = [(qr * fr - qi * fi, qr * fi + qi * fr) for fr, fi in patches]
    turned = []
    for k, w, (zr, zi) in zip(slots, live, transforms(waves, left, right)):
        power = zr * zr + zi * zi
        ratio = (amplitude[k] * lax.rsqrt(jnp.maximum(power, amp_floor * amp_floor)) - 1.0) * w
        turned.append((zr * ratio, -(zi * ratio)))
    sums = [0.0, 0.0, 0.0]
    for w, (r, c), (fr, fi), (br, bi) in zip(live, at, patches, transforms(turned, left, right)):
        sums[0] = sums[0] + (fr * br - fi * bi)
        sums[1] = sums[1] - (fr * bi + fi * br)
        sums[2] = sums[2] + (fr * fr + fi * fi) * w
        deposit(canvas, (0,), r, c, qr * br - qi * bi)
        deposit(canvas, (1,), r, c, -(qr * bi) - qi * br)
    for p in range(3):
        grads[p] += sums[p]


def near_frames(infos, listed):
    total = jnp.int32(0)
    for a in range(3):
        for b in range(3):
            for k in range(4):
                r = infos[a][b, k] + (TILE * a - (TILE - F))
                c = infos[a][b, 4 + k] + (TILE * b - (TILE - F))
                use = (k < infos[a][b, 8]) & (r > 0) & (r < F + WIDE) & (c > 0) & (c < F + WIDE)
                listed[0, total] = r
                listed[1, total] = c
                total = total + use.astype(jnp.int32)
    return total


def visit_frames(mine, infos, amplitude, left, right, ob, pr, canvas, glow, grads, listed):
    n = near_frames(infos, listed)
    canvas[...] = jnp.zeros_like(canvas)
    glow[F : F + WIDE, F : F + WIDE] = jnp.zeros((WIDE, WIDE), jnp.float32)
    light = pr[0] * pr[0] + pr[1] * pr[1]

    def shine(i):
        used = (i < n).astype(jnp.float32)
        at = jnp.where(i < n, i, 0)
        deposit(glow, (), listed[0, at], listed[1, at], light * used)

    grads[...] = jnp.zeros_like(grads)

    def pair(i, carry):
        visit_pair(i, mine, amplitude, left, right, ob, pr, canvas, grads)
        for j in range(BESIDE):
            shine(i * BESIDE + j)
        return carry

    pairs = (mine[0, 8] + 1) // 2
    lax.fori_loop(0, pairs, pair, 0)

    def more(i, carry):
        shine(i)
        return carry

    lax.fori_loop(pairs * BESIDE, n, more, 0)


def hand_out(canvas, grads, zl_out, zr_out, up_out, mid_out, dn_out, g_out):
    zl_out[...] = canvas[:, :, :F]
    zr_out[...] = canvas[:, :, TILE:]
    up_out[:2] = canvas[:, :F, F:TILE]
    mid_out[...] = canvas[:, F:TILE, F:TILE]
    dn_out[:2] = canvas[:, TILE:, F:TILE]
    for p in range(3):
        for h in range(2):
            for t in range(2):
                g_out[pl.ds(4 * p + 2 * t + h, HALF, stride=12), :] = grads[p, h * HALF : (h + 1) * HALF, t * LANES : (t + 1) * LANES]


def start_kernel(tile, probe, ob, pr, own):
    ob[:, :TILE, :TILE] = tile[...]
    pr[...] = probe[...]
    me = lax.axis_index("row") * lax.axis_size("col") + lax.axis_index("col")
    picked = lax.broadcasted_iota(jnp.int32, (HALF, LANES), 0) == me
    rows = []
    for p in range(2):
        for t in range(2):
            for h in range(2):
                rows.append(jnp.sum(jnp.where(picked, probe[p, h * HALF : (h + 1) * HALF, t * LANES : (t + 1) * LANES], 0.0), axis=0, keepdims=True))
    own[...] = jnp.concatenate(rows, 0)


def first_kernel(mine, ia, ib, ic, amp, left, right, pr, tile, below, below_right, beside, corner, *rest):
    ob, light, outs, (unused, canvas, grads, listed, glow) = rest[0], rest[1], rest[2:8], rest[8:]
    ob[:, TILE:, :F] = below[...]
    ob[:, TILE:, F:TILE] = below_right[...]
    ob[:, :TILE, TILE:] = beside[...]
    ob[:, TILE:, TILE:] = corner[...]
    visit_frames(mine, (ia, ib, ic), amp, left, right, ob, pr, canvas, glow, grads, listed)
    light[...] = glow[F : F + WIDE, F : F + WIDE]
    hand_out(canvas, grads, *outs)


def gathered_probe(pg, pr):
    for p in range(2):
        for h in range(2):
            for t in range(2):
                pr[p, h * HALF : (h + 1) * HALF, t * LANES : (t + 1) * LANES] = pg[pl.ds(4 * p + 2 * t + h, HALF, stride=8), :]


def refreshed(put, size, o, l, zl, zr, up, mid, dn, left_in, right_in, cup, cdn, sup, sdn):
    for i in range(size // F):
        for j in range(size // F):
            for at in range(0, F, STRIP):
                here = slice(at, at + STRIP)
                rows, cols = slice(i * F + at, i * F + at + STRIP), slice(j * F, (j + 1) * F)
                scale = 1.0 / (l[rows, cols] + object_damping)
                for p in range(2):
                    if j == 0:
                        s = zl[p, rows, :] + left_in[p, rows, :]
                    elif j == 1:
                        s = (up, mid, dn)[i][p, here, :]
                    else:
                        s = zr[p, rows, :] + right_in[p, rows, :]
                    if i == 0:
                        s = s + (cdn[p, here, :] if j == 1 else sdn[j // 2, p, here, :])
                    if i == 2:
                        s = s + (cup[p, here, :] if j == 1 else sup[j // 2, p, here, :])
                    put(p, rows, cols, o[p, rows, cols] + s * scale)


def next_kernel(mine, ia, ib, ic, amp, left, right, pg, o, l, zl, zr, up, mid, dn, left_in, right_in, cup, cdn, sup, sdn, *rest):
    ob, light, outs, (pr, canvas, grads, listed, glow) = rest[0], rest[1], rest[2:8], rest[8:]

    def put(p, rows, cols, value):
        ob[p, rows, cols] = value

    refreshed(put, WIDE, o, l, zl, zr, up, mid, dn, left_in, right_in, cup, cdn, sup, sdn)
    gathered_probe(pg, pr)
    visit_frames(mine, (ia, ib, ic), amp, left, right, ob, pr, canvas, glow, grads, listed)
    light[...] = glow[F : F + WIDE, F : F + WIDE]
    hand_out(canvas, grads, *outs)


def last_kernel(pg, o, l, zl, up, mid, left_in, cdn, sdn, o_out, p_out):
    def put(p, rows, cols, value):
        o_out[p, rows, cols] = value

    refreshed(put, TILE, o, l, zl, None, up, mid, None, left_in, None, None, cdn, None, sdn)
    gathered_probe(pg, p_out)


def middle_kernel(last, g, old, zl, left_in, *rest):
    if last:
        sdn, new, spread = rest
        sdn[0] = zl[:, TILE:] + left_in[:, TILE:]
    else:
        zr, right_in, sup, sdn, new, spread = rest
        sup[0] = zl[:, :F] + left_in[:, :F]
        sup[1] = zr[:, :F] + right_in[:, :F]
        sdn[0] = zl[:, TILE:] + left_in[:, TILE:]
        sdn[1] = zr[:, TILE:] + right_in[:, TILE:]
    s = jnp.sum(g[...].reshape(HALF // 2, 24, LANES), axis=0)
    s = s[:12] + s[12:]
    value = old[...] + s[:8] / (jnp.concatenate([s[8:], s[8:]], 0) + probe_damping)
    new[...] = value
    spread[...] = jnp.broadcast_to(value[None], (HALF, 8, LANES)).reshape(HALF * 8, LANES)


def f32(*shape):
    return jax.ShapeDtypeStruct(shape, jnp.float32)


def call(kernel, args, outs, scratch=(), limit=14, smem=(), cost=None, alias=None):
    return pl.pallas_call(
        kernel,
        out_shape=tuple(outs),
        in_specs=[SMEM if i in smem else VMEM for i in range(len(args))],
        out_specs=tuple(VMEM for _ in outs),
        scratch_shapes=list(scratch),
        compiler_params=pltpu.CompilerParams(vmem_limit_bytes=limit << 20),
        cost_estimate=cost,
        input_output_aliases=alias or {},
    )(*args)


def call_frames(kernel, *args, alias=None):
    scratch = [
        pltpu.VMEM((2, F, F), jnp.float32),
        pltpu.VMEM((2, WIDE, WIDE), jnp.float32),
        pltpu.VMEM((3, F, F), jnp.float32),
        pltpu.SMEM((2, 40), jnp.int32),
        pltpu.VMEM((WIDE + 2 * F, WIDE + 2 * F), jnp.float32),
    ]
    outs = (
        f32(2, WIDE, WIDE), f32(WIDE, WIDE), f32(2, WIDE, F), f32(2, WIDE, F),
        f32(3, F, F), f32(2, F, F), f32(3, F, F), f32(HALF * 12, LANES),
    )
    return call(kernel, args, outs, scratch, limit=FRAMES_LIMIT, smem=(0, 1, 2, 3), alias=alias)


def everyone(x):
    return lax.all_to_all(x, ("row", "col"), 0, 0)


def shards(object_field, probe, amplitude, positions, counts):
    left, right = (jnp.asarray(t) for t in tables())
    amp = amplitude[0, 0]
    mine = jnp.concatenate([positions[0, 0, :, 0], positions[0, 0, :, 1], counts[0], jnp.zeros((7,), jnp.int32)])[None]

    below = passed_along(object_field[:, :F, :F], "row", -1)
    beside = passed_along(object_field[:, :, :F], "col", -1)
    below_right = passed_along(object_field[:, :F, F:], "row", -1)
    info = jnp.concatenate([passed_along(mine, "col", 1), mine, passed_along(mine, "col", -1)], 0)
    below, info = lax.optimization_barrier((below, info))
    infos = (passed_along(info, "row", 1), info, passed_along(info, "row", -1))
    corner = passed_along(below, "col", -1)
    wide, probe, own = call(start_kernel, (object_field, probe), (f32(2, WIDE, WIDE), f32(2, F, F), f32(8, LANES)))

    state = call_frames(
        first_kernel, mine, *infos, amp, left, right, probe, wide, below, below_right, beside, corner, alias={8: 0},
    )
    for sweep in range(PASSES):
        last = sweep == PASSES - 1
        ob, light, to_left, to_right, up, mid, down, grad = state
        grad = grad.reshape(HALF, 3, 4, LANES)
        from_left = passed_along(to_right, "col", 1)
        centre_down = passed_along(down, "row", 1)
        moved = [from_left, centre_down]
        if not last:
            moved += [passed_along(to_left, "col", -1), passed_along(up, "row", -1)]
        grad, to_left, to_right = lax.optimization_barrier((grad, to_left, to_right))
        grad = everyone(grad)
        grad, moved = lax.optimization_barrier((grad, moved))
        grad = grad.reshape(HALF * 12, LANES)
        tail = (f32(8, LANES), f32(HALF * 8, LANES))
        if last:
            from_left, centre_down = moved
            side_down, own, spread = call(
                lambda *refs: middle_kernel(True, *refs), (grad, own, to_left, from_left), (f32(1, 2, F, F),) + tail,
            )
            sides = (side_down,)
            moved = (passed_along(side_down, "row", 1),)
        else:
            from_left, centre_down, from_right, centre_up = moved
            side_up, side_down, own, spread = call(
                lambda *refs: middle_kernel(False, *refs), (grad, own, to_left, from_left, to_right, from_right),
                (f32(2, 2, F, F), f32(2, 2, F, F)) + tail,
            )
            sides = (side_up, side_down)
            moved = (passed_along(side_up, "row", -1), passed_along(side_down, "row", 1))
        sides, spread = lax.optimization_barrier((sides, spread))
        pg = everyone(spread.reshape(HALF, 2, 4, LANES)).reshape(HALF * 8, LANES)
        if last:
            return call(
                last_kernel, (pg, ob, light, to_left, up, mid, from_left, centre_down, moved[0]),
                (f32(2, TILE, TILE), f32(2, F, F)),
            )
        state = call_frames(
            next_kernel, mine, *infos, amp, left, right, pg, ob, light, to_left, to_right, up, mid, down,
            from_left, from_right, centre_up, centre_down, moved[0], moved[1], alias={8: 0},
        )


def solution(mesh):
    return jax.shard_map(
        shards,
        mesh=mesh,
        in_specs=(
            P(None, "row", "col"),
            P(),
            P("row", "col", None, None, None),
            P("row", "col", None, None),
            P("row", "col"),
        ),
        out_specs=(P(None, "row", "col"), P()),
        check_vma=False,
    )
```

```python
import math

import jax
import jax.numpy as jnp
import numpy as np
from jax import lax
from jax.experimental import pallas as pl
from jax.experimental.pallas import tpu as pltpu
from jax.sharding import PartitionSpec as P

PASSES = 3
F = 256
TILE = 512
WIDE = TILE + F
HALF = F // 2
LANES = 128
FRAMES_LIMIT = 22
BESIDE = 6
STRIP = 32

amp_floor = 0.1
object_damping = 0.5
probe_damping = 1.0

VMEM = pl.BlockSpec(memory_space=pltpu.VMEM)
SMEM = pl.BlockSpec(memory_space=pltpu.SMEM)


def passed_along(block, axis, distance):
    size = lax.axis_size(axis)
    route = [((i - distance) % size, i) for i in range(size)]
    return lax.ppermute(block, axis, route)


def split(x):
    high = x.astype(jnp.bfloat16)
    low = (x - high.astype(jnp.float32)).astype(jnp.bfloat16)
    return high, low


def tables():
    k = np.arange(F)
    angles = (k[:, None] * k[None, :] % F) * (-2.0 * math.pi / F)
    re = np.cos(angles) / math.sqrt(F)
    im = np.sin(angles) / math.sqrt(F)
    left = np.block([[re, -im], [im, re]]).astype(np.float32)
    right = np.block([[re, im], [-im, re]]).astype(np.float32)

    def terms(m):
        high = m.astype(jnp.bfloat16)
        low = (m - high.astype(np.float32)).astype(jnp.bfloat16)
        return high, low

    lh, ll = terms(left)
    rh, rl = terms(right)
    return np.concatenate([lh, lh, ll], 1), np.concatenate([rh, rh, rl], 0)


def stacked(re, im):
    h, l = split(jnp.concatenate([re, im], 0))
    return jnp.concatenate([h, l, h], 0)


def abreast(y):
    h, l = split(jnp.concatenate([y[:F], y[F:]], 1))
    return jnp.concatenate([h, l, h], 1)


def transforms(fields, left, right):
    ys = [jnp.dot(left[...], stacked(re, im), preferred_element_type=jnp.float32) for re, im in fields]
    zs = [jnp.dot(abreast(y), right[...], preferred_element_type=jnp.float32) for y in ys]
    return [(z[:, :F], z[:, F:]) for z in zs]


def window(ref, lead, r, c):
    r0 = pl.multiple_of((r // 8) * 8, 8)
    c0 = pl.multiple_of((c // LANES) * LANES, LANES)
    rs, cs = r - r0, c - c0
    w = ref[lead + (pl.ds(r0, F + 8), pl.ds(c0, F + LANES))]
    lane = lax.broadcasted_iota(jnp.int32, (F + 8, LANES), 1)
    back = lax.rem(LANES - cs, LANES)
    t = [pltpu.roll(w[:, i * LANES : (i + 1) * LANES], back, 1) for i in range(3)]
    w = jnp.concatenate([jnp.where(lane < LANES - cs, t[i], t[i + 1]) for i in range(2)], 1)
    w = pltpu.roll(w.reshape(F // 8 + 1, 8, F), lax.rem(8 - rs, 8), 1)
    sub = lax.broadcasted_iota(jnp.int32, (F // 8, 8, F), 1)
    return jnp.where(sub < 8 - rs, w[:-1], w[1:]).reshape(F, F)


def deposit(ref, lead, r, c, x):
    r0 = pl.multiple_of((r // 8) * 8, 8)
    c0 = pl.multiple_of((c // LANES) * LANES, LANES)
    rs, cs = r - r0, c - c0
    w = pltpu.roll(x.reshape(F // 8, 8, F), rs, 1)
    zero = jnp.zeros((1, 8, F), jnp.float32)
    sub = lax.broadcasted_iota(jnp.int32, (F // 8 + 1, 8, F), 1)
    w = jnp.where(sub >= rs, jnp.concatenate([w, zero], 0), jnp.concatenate([zero, w], 0))
    w = w.reshape(F + 8, F)
    lane = lax.broadcasted_iota(jnp.int32, (F + 8, LANES), 1)
    a = pltpu.roll(w[:, :LANES], cs, 1)
    b = pltpu.roll(w[:, LANES:], cs, 1)
    t = [jnp.where(lane >= cs, a, 0.0), jnp.where(lane >= cs, b, a), jnp.where(lane >= cs, 0.0, b)]
    at = lead + (pl.ds(r0, F + 8), pl.ds(c0, F + LANES))
    ref[at] = ref[at] + jnp.concatenate(t, 1)


def visit_pair(i, mine, amplitude, left, right, ob, pr, canvas, grads):
    slots = (2 * i, 2 * i + 1)
    live = (1.0, (2 * i + 1 < mine[0, 8]).astype(jnp.float32))
    at = [(mine[0, k], mine[0, 4 + k]) for k in slots]
    patches = [[window(ob, (p,), r, c) for p in range(2)] for r, c in at]
    qr, qi = pr[0], pr[1]
    waves = [(qr * fr - qi * fi, qr * fi + qi * fr) for fr, fi in patches]
    turned = []
    for k, w, (zr, zi) in zip(slots, live, transforms(waves, left, right)):
        power = zr * zr + zi * zi
        ratio = (amplitude[k] * lax.rsqrt(jnp.maximum(power, amp_floor * amp_floor)) - 1.0) * w
        turned.append((zr * ratio, -(zi * ratio)))
    sums = [0.0, 0.0, 0.0]
    for w, (r, c), (fr, fi), (br, bi) in zip(live, at, patches, transforms(turned, left, right)):
        sums[0] = sums[0] + (fr * br - fi * bi)
        sums[1] = sums[1] - (fr * bi + fi * br)
        sums[2] = sums[2] + (fr * fr + fi * fi) * w
        deposit(canvas, (0,), r, c, qr * br - qi * bi)
        deposit(canvas, (1,), r, c, -(qr * bi) - qi * br)
    for p in range(3):
        grads[p] += sums[p]


def near_frames(infos, listed):
    total = jnp.int32(0)
    for a in range(3):
        for b in range(3):
            for k in range(4):
                r = infos[a][b, k] + (TILE * a - (TILE - F))
                c = infos[a][b, 4 + k] + (TILE * b - (TILE - F))
                use = (k < infos[a][b, 8]) & (r > 0) & (r < F + WIDE) & (c > 0) & (c < F + WIDE)
                listed[0, total] = r
                listed[1, total] = c
                total = total + use.astype(jnp.int32)
    return total


def visit_frames(mine, infos, amplitude, left, right, ob, pr, canvas, glow, grads, listed):
    n = near_frames(infos, listed)
    canvas[...] = jnp.zeros_like(canvas)
    glow[F : F + WIDE, F : F + WIDE] = jnp.zeros((WIDE, WIDE), jnp.float32)
    light = pr[0] * pr[0] + pr[1] * pr[1]

    def shine(i):
        used = (i < n).astype(jnp.float32)
        at = jnp.where(i < n, i, 0)
        deposit(glow, (), listed[0, at], listed[1, at], light * used)

    grads[...] = jnp.zeros_like(grads)

    def pair(i, carry):
        visit_pair(i, mine, amplitude, left, right, ob, pr, canvas, grads)
        for j in range(BESIDE):
            shine(i * BESIDE + j)
        return carry

    pairs = (mine[0, 8] + 1) // 2
    lax.fori_loop(0, pairs, pair, 0)

    def more(i, carry):
        shine(i)
        return carry

    lax.fori_loop(pairs * BESIDE, n, more, 0)


def on_left_core():
    return lax.rem(lax.axis_index("col"), 2) == 0


def hand_out(canvas, grads, zl_out, zr_out, up_out, mid_out, dn_out, g_out):
    zl_out[...] = canvas[:, :, :F]
    zr_out[...] = canvas[:, :, TILE:]
    up_out[:2] = canvas[:, :F, F:TILE]
    up_out[2] = jnp.where(on_left_core(), canvas[0, :F, TILE:], canvas[0, :F, :F])
    mid_out[...] = canvas[:, F:TILE, F:TILE]
    dn_out[:2] = canvas[:, TILE:, F:TILE]
    dn_out[2] = jnp.where(on_left_core(), canvas[0, TILE:, TILE:], canvas[0, TILE:, :F])
    for p in range(3):
        for h in range(2):
            for t in range(2):
                g_out[pl.ds(4 * p + 2 * t + h, HALF, stride=12), :] = grads[p, h * HALF : (h + 1) * HALF, t * LANES : (t + 1) * LANES]


def start_kernel(tile, probe, ob, pr, own):
    ob[:, :TILE, :TILE] = tile[...]
    pr[...] = probe[...]
    me = lax.axis_index("row") * lax.axis_size("col") + lax.axis_index("col")
    picked = lax.broadcasted_iota(jnp.int32, (HALF, LANES), 0) == me
    rows = []
    for p in range(2):
        for t in range(2):
            for h in range(2):
                rows.append(jnp.sum(jnp.where(picked, probe[p, h * HALF : (h + 1) * HALF, t * LANES : (t + 1) * LANES], 0.0), axis=0, keepdims=True))
    own[...] = jnp.concatenate(rows, 0)


def first_kernel(mine, ia, ib, ic, amp, left, right, pr, tile, below, below_right, beside, corner, *rest):
    ob, light, outs, (unused, canvas, grads, listed, glow) = rest[0], rest[1], rest[2:8], rest[8:]
    ob[:, TILE:, :F] = below[...]
    ob[:, TILE:, F:TILE] = below_right[...]
    ob[:, :TILE, TILE:] = beside[...]
    ob[:, TILE:, TILE:] = corner[...]
    visit_frames(mine, (ia, ib, ic), amp, left, right, ob, pr, canvas, glow, grads, listed)
    light[...] = glow[F : F + WIDE, F : F + WIDE]
    hand_out(canvas, grads, *outs)


def gathered_probe(pg, pr):
    for p in range(2):
        for h in range(2):
            for t in range(2):
                pr[p, h * HALF : (h + 1) * HALF, t * LANES : (t + 1) * LANES] = pg[pl.ds(4 * p + 2 * t + h, HALF, stride=8), :]


def refreshed(put, size, o, l, zl, zr, up, mid, dn, left_in, right_in, across):
    for i in range(size // F):
        for j in range(size // F):
            for at in range(0, F, STRIP):
                here = slice(at, at + STRIP)
                rows, cols = slice(i * F + at, i * F + at + STRIP), slice(j * F, (j + 1) * F)
                scale = 1.0 / (l[rows, cols] + object_damping)
                for p in range(2):
                    if j == 0:
                        s = zl[p, rows, :] + left_in[p, rows, :]
                    elif j == 1:
                        s = (up, mid, dn)[i][p, here, :]
                    else:
                        s = zr[p, rows, :] + right_in[p, rows, :]
                    if i != 1:
                        s = s + across(i, j, p, here)
                    put(p, rows, cols, o[p, rows, cols] + s * scale)


def next_kernel(mine, ia, ib, ic, amp, left, right, pg, o, l, zl, zr, up, mid, dn, left_in, right_in, cup, cdn, sup, sdn, swap, *rest):
    ob, light, outs, (pr, canvas, grads, listed, glow) = rest[0], rest[1], rest[2:8], rest[8:]

    def put(p, rows, cols, value):
        ob[p, rows, cols] = value

    left_core = on_left_core()

    def across(i, j, p, here):
        centre, side = (cdn, sdn) if i == 0 else (cup, sup)
        if j == 1:
            return centre[p, here, :]
        outer = side[p, here, :]
        inner = centre[2, here, :] + swap[i // 2, here, :] if p == 0 else side[2, here, :]
        return jnp.where(left_core == (j == 2), inner, outer)

    refreshed(put, WIDE, o, l, zl, zr, up, mid, dn, left_in, right_in, across)
    gathered_probe(pg, pr)
    visit_frames(mine, (ia, ib, ic), amp, left, right, ob, pr, canvas, glow, grads, listed)
    light[...] = glow[F : F + WIDE, F : F + WIDE]
    hand_out(canvas, grads, *outs)


def last_kernel(pg, o, l, zl, up, mid, left_in, cdn, sdn, o_out, p_out):
    def put(p, rows, cols, value):
        o_out[p, rows, cols] = value

    def across(i, j, p, here):
        return cdn[p, here, :] if j == 1 else sdn[0, p, here, :]

    refreshed(put, TILE, o, l, zl, None, up, mid, None, left_in, None, across)
    gathered_probe(pg, p_out)


def middle_kernel(last, g, old, zl, left_in, *rest):
    if last:
        sdn, new, spread = rest
        sdn[0] = zl[:, TILE:] + left_in[:, TILE:]
    else:
        zr, right_in, cup, cdn, sup, sdn, swap, new, spread = rest
        left_core = on_left_core()
        for out, rows in ((sup, slice(0, F)), (sdn, slice(TILE, WIDE))):
            for p in range(2):
                a = zl[p, rows] + left_in[p, rows]
                b = zr[p, rows] + right_in[p, rows]
                out[p] = jnp.where(left_core, a, b)
                if p == 1:
                    out[2] = jnp.where(left_core, b, a)
        swap[0] = cdn[2]
        swap[1] = cup[2]
    s = jnp.sum(g[...].reshape(HALF // 2, 24, LANES), axis=0)
    s = s[:12] + s[12:]
    value = old[...] + s[:8] / (jnp.concatenate([s[8:], s[8:]], 0) + probe_damping)
    new[...] = value
    spread[...] = jnp.broadcast_to(value[None], (HALF, 8, LANES)).reshape(HALF * 8, LANES)


def f32(*shape):
    return jax.ShapeDtypeStruct(shape, jnp.float32)


def call(kernel, args, outs, scratch=(), limit=14, smem=(), cost=None, alias=None):
    return pl.pallas_call(
        kernel,
        out_shape=tuple(outs),
        in_specs=[SMEM if i in smem else VMEM for i in range(len(args))],
        out_specs=tuple(VMEM for _ in outs),
        scratch_shapes=list(scratch),
        compiler_params=pltpu.CompilerParams(vmem_limit_bytes=limit << 20),
        cost_estimate=cost,
        input_output_aliases=alias or {},
    )(*args)


def call_frames(kernel, *args, alias=None):
    scratch = [
        pltpu.VMEM((2, F, F), jnp.float32),
        pltpu.VMEM((2, WIDE, WIDE), jnp.float32),
        pltpu.VMEM((3, F, F), jnp.float32),
        pltpu.SMEM((2, 40), jnp.int32),
        pltpu.VMEM((WIDE + 2 * F, WIDE + 2 * F), jnp.float32),
    ]
    outs = (
        f32(2, WIDE, WIDE), f32(WIDE, WIDE), f32(2, WIDE, F), f32(2, WIDE, F),
        f32(3, F, F), f32(2, F, F), f32(3, F, F), f32(HALF * 12, LANES),
    )
    return call(kernel, args, outs, scratch, limit=FRAMES_LIMIT, smem=(0, 1, 2, 3), alias=alias)


def everyone(x):
    return lax.all_to_all(x, ("row", "col"), 0, 0)


def shards(object_field, probe, amplitude, positions, counts):
    left, right = (jnp.asarray(t) for t in tables())
    amp = amplitude[0, 0]
    mine = jnp.concatenate([positions[0, 0, :, 0], positions[0, 0, :, 1], counts[0], jnp.zeros((7,), jnp.int32)])[None]

    below = passed_along(object_field[:, :F, :F], "row", -1)
    beside = passed_along(object_field[:, :, :F], "col", -1)
    below_right = passed_along(object_field[:, :F, F:], "row", -1)
    info = jnp.concatenate([passed_along(mine, "col", 1), mine, passed_along(mine, "col", -1)], 0)
    below, info = lax.optimization_barrier((below, info))
    infos = (passed_along(info, "row", 1), info, passed_along(info, "row", -1))
    corner = passed_along(below, "col", -1)
    wide, probe, own = call(start_kernel, (object_field, probe), (f32(2, WIDE, WIDE), f32(2, F, F), f32(8, LANES)))

    state = call_frames(
        first_kernel, mine, *infos, amp, left, right, probe, wide, below, below_right, beside, corner, alias={8: 0},
    )
    for sweep in range(PASSES):
        last = sweep == PASSES - 1
        ob, light, to_left, to_right, up, mid, down, grad = state
        grad = grad.reshape(HALF, 3, 4, LANES)
        from_left = passed_along(to_right, "col", 1)
        centre_down = passed_along(down, "row", 1)
        moved = [from_left, centre_down]
        if not last:
            moved += [passed_along(to_left, "col", -1), passed_along(up, "row", -1)]
        grad, to_left, to_right = lax.optimization_barrier((grad, to_left, to_right))
        grad = everyone(grad)
        grad, moved = lax.optimization_barrier((grad, moved))
        grad = grad.reshape(HALF * 12, LANES)
        tail = (f32(8, LANES), f32(HALF * 8, LANES))
        if last:
            from_left, centre_down = moved
            side_down, own, spread = call(
                lambda *refs: middle_kernel(True, *refs), (grad, own, to_left, from_left), (f32(1, 2, F, F),) + tail,
            )
            sides = (side_down,)
            moved = (passed_along(side_down, "row", 1),)
        else:
            from_left, centre_down, from_right, centre_up = moved
            side_up, side_down, swap, own, spread = call(
                lambda *refs: middle_kernel(False, *refs),
                (grad, own, to_left, from_left, to_right, from_right, centre_up, centre_down),
                (f32(3, F, F), f32(3, F, F), f32(2, F, F)) + tail,
            )
            sides = (side_up, side_down, swap)
            swapped = lax.ppermute(swap, "col", [(i, i ^ 1) for i in range(lax.axis_size("col"))])
            moved = (passed_along(side_up, "row", -1), passed_along(side_down, "row", 1), swapped)
        sides, spread = lax.optimization_barrier((sides, spread))
        pg = everyone(spread.reshape(HALF, 2, 4, LANES)).reshape(HALF * 8, LANES)
        if last:
            return call(
                last_kernel, (pg, ob, light, to_left, up, mid, from_left, centre_down, moved[0]),
                (f32(2, TILE, TILE), f32(2, F, F)),
            )
        state = call_frames(
            next_kernel, mine, *infos, amp, left, right, pg, ob, light, to_left, to_right, up, mid, down,
            from_left, from_right, centre_up, centre_down, *moved, alias={8: 0},
        )


def solution(mesh):
    return jax.shard_map(
        shards,
        mesh=mesh,
        in_specs=(
            P(None, "row", "col"),
            P(),
            P("row", "col", None, None, None),
            P("row", "col", None, None),
            P("row", "col"),
        ),
        out_specs=(P(None, "row", "col"), P()),
        check_vma=False,
    )
```

```python
import math

import jax
import jax.numpy as jnp
import numpy as np
from jax import lax
from jax.experimental import pallas as pl
from jax.experimental.pallas import tpu as pltpu
from jax.sharding import PartitionSpec as P

PASSES = 3
F = 256
TILE = 512
WIDE = TILE + F
HALF = F // 2
PART = F // 4
LANES = 128
FRAMES_LIMIT = 22
BESIDE = 6
STRIP = 32

amp_floor = 0.1
object_damping = 0.5
probe_damping = 1.0

VMEM = pl.BlockSpec(memory_space=pltpu.VMEM)
SMEM = pl.BlockSpec(memory_space=pltpu.SMEM)


def passed_along(block, axis, distance):
    size = lax.axis_size(axis)
    route = [((i - distance) % size, i) for i in range(size)]
    return lax.ppermute(block, axis, route)


def split(x):
    high = x.astype(jnp.bfloat16)
    low = (x - high.astype(jnp.float32)).astype(jnp.bfloat16)
    return high, low


def tables():
    k = np.arange(F)
    angles = (k[:, None] * k[None, :] % F) * (-2.0 * math.pi / F)
    re = np.cos(angles) / math.sqrt(F)
    im = np.sin(angles) / math.sqrt(F)
    left = np.block([[re, -im], [im, re]]).astype(np.float32)
    right = np.block([[re, im], [-im, re]]).astype(np.float32)

    def terms(m):
        high = m.astype(jnp.bfloat16)
        low = (m - high.astype(np.float32)).astype(jnp.bfloat16)
        return high, low

    lh, ll = terms(left)
    rh, rl = terms(right)
    return np.concatenate([lh, lh, ll], 1), np.concatenate([rh, rh, rl], 0)


def stacked(re, im):
    h, l = split(jnp.concatenate([re, im], 0))
    return jnp.concatenate([h, l, h], 0)


def abreast(y):
    h, l = split(jnp.concatenate([y[:F], y[F:]], 1))
    return jnp.concatenate([h, l, h], 1)


def transforms(fields, left, right):
    ys = [jnp.dot(left[...], stacked(re, im), preferred_element_type=jnp.float32) for re, im in fields]
    zs = [jnp.dot(abreast(y), right[...], preferred_element_type=jnp.float32) for y in ys]
    return [(z[:, :F], z[:, F:]) for z in zs]


def window(ref, lead, r, c):
    r0 = pl.multiple_of((r // 8) * 8, 8)
    c0 = pl.multiple_of((c // LANES) * LANES, LANES)
    rs, cs = r - r0, c - c0
    w = ref[lead + (pl.ds(r0, F + 8), pl.ds(c0, F + LANES))]
    lane = lax.broadcasted_iota(jnp.int32, (F + 8, LANES), 1)
    back = lax.rem(LANES - cs, LANES)
    t = [pltpu.roll(w[:, i * LANES : (i + 1) * LANES], back, 1) for i in range(3)]
    w = jnp.concatenate([jnp.where(lane < LANES - cs, t[i], t[i + 1]) for i in range(2)], 1)
    w = pltpu.roll(w.reshape(F // 8 + 1, 8, F), lax.rem(8 - rs, 8), 1)
    sub = lax.broadcasted_iota(jnp.int32, (F // 8, 8, F), 1)
    return jnp.where(sub < 8 - rs, w[:-1], w[1:]).reshape(F, F)


def deposit(ref, lead, r, c, x):
    r0 = pl.multiple_of((r // 8) * 8, 8)
    c0 = pl.multiple_of((c // LANES) * LANES, LANES)
    rs, cs = r - r0, c - c0
    w = pltpu.roll(x.reshape(F // 8, 8, F), rs, 1)
    zero = jnp.zeros((1, 8, F), jnp.float32)
    sub = lax.broadcasted_iota(jnp.int32, (F // 8 + 1, 8, F), 1)
    w = jnp.where(sub >= rs, jnp.concatenate([w, zero], 0), jnp.concatenate([zero, w], 0))
    w = w.reshape(F + 8, F)
    lane = lax.broadcasted_iota(jnp.int32, (F + 8, LANES), 1)
    a = pltpu.roll(w[:, :LANES], cs, 1)
    b = pltpu.roll(w[:, LANES:], cs, 1)
    t = [jnp.where(lane >= cs, a, 0.0), jnp.where(lane >= cs, b, a), jnp.where(lane >= cs, 0.0, b)]
    at = lead + (pl.ds(r0, F + 8), pl.ds(c0, F + LANES))
    ref[at] = ref[at] + jnp.concatenate(t, 1)


def visit_pair(i, mine, amplitude, left, right, ob, pr, canvas, grads):
    slots = (2 * i, 2 * i + 1)
    live = (1.0, (2 * i + 1 < mine[0, 8]).astype(jnp.float32))
    at = [(mine[0, k], mine[0, 4 + k]) for k in slots]
    patches = [[window(ob, (p,), r, c) for p in range(2)] for r, c in at]
    qr, qi = pr[0], pr[1]
    waves = [(qr * fr - qi * fi, qr * fi + qi * fr) for fr, fi in patches]
    turned = []
    for k, w, (zr, zi) in zip(slots, live, transforms(waves, left, right)):
        power = zr * zr + zi * zi
        ratio = (amplitude[k] * lax.rsqrt(jnp.maximum(power, amp_floor * amp_floor)) - 1.0) * w
        turned.append((zr * ratio, -(zi * ratio)))
    sums = [0.0, 0.0, 0.0]
    for w, (r, c), (fr, fi), (br, bi) in zip(live, at, patches, transforms(turned, left, right)):
        sums[0] = sums[0] + (fr * br - fi * bi)
        sums[1] = sums[1] - (fr * bi + fi * br)
        sums[2] = sums[2] + (fr * fr + fi * fi) * w
        deposit(canvas, (0,), r, c, qr * br - qi * bi)
        deposit(canvas, (1,), r, c, -(qr * bi) - qi * br)
    for p in range(3):
        grads[p] += sums[p]


def near_frames(infos, listed):
    total = jnp.int32(0)
    for a in range(3):
        for b in range(3):
            for k in range(4):
                r = infos[a][b, k] + (TILE * a - (TILE - F))
                c = infos[a][b, 4 + k] + (TILE * b - (TILE - F))
                use = (k < infos[a][b, 8]) & (r > 0) & (r < F + WIDE) & (c > 0) & (c < F + WIDE)
                listed[0, total] = r
                listed[1, total] = c
                total = total + use.astype(jnp.int32)
    return total


def visit_frames(mine, infos, amplitude, left, right, ob, pr, canvas, glow, grads, listed):
    n = near_frames(infos, listed)
    canvas[...] = jnp.zeros_like(canvas)
    glow[F : F + WIDE, F : F + WIDE] = jnp.zeros((WIDE, WIDE), jnp.float32)
    light = pr[0] * pr[0] + pr[1] * pr[1]

    def shine(i):
        used = (i < n).astype(jnp.float32)
        at = jnp.where(i < n, i, 0)
        deposit(glow, (), listed[0, at], listed[1, at], light * used)

    grads[...] = jnp.zeros_like(grads)

    def pair(i, carry):
        visit_pair(i, mine, amplitude, left, right, ob, pr, canvas, grads)
        for j in range(BESIDE):
            shine(i * BESIDE + j)
        return carry

    pairs = (mine[0, 8] + 1) // 2
    lax.fori_loop(0, pairs, pair, 0)

    def more(i, carry):
        shine(i)
        return carry

    lax.fori_loop(pairs * BESIDE, n, more, 0)


def on_left_core():
    return lax.rem(lax.axis_index("col"), 2) == 0


def hand_out(canvas, grads, zl_out, zr_out, up_out, mid_out, dn_out, keep_out, send_out):
    zl_out[...] = canvas[:, :, :F]
    zr_out[...] = canvas[:, :, TILE:]
    up_out[:2] = canvas[:, :F, F:TILE]
    up_out[2] = jnp.where(on_left_core(), canvas[0, :F, TILE:], canvas[0, :F, :F])
    mid_out[...] = canvas[:, F:TILE, F:TILE]
    dn_out[:2] = canvas[:, TILE:, F:TILE]
    dn_out[2] = jnp.where(on_left_core(), canvas[0, TILE:, TILE:], canvas[0, TILE:, :F])
    left_core = on_left_core()
    for p in range(3):
        for h in range(2):
            for t in range(2):
                a, b = (grads[p, (2 * k + h) * PART : (2 * k + h + 1) * PART, t * LANES : (t + 1) * LANES] for k in range(2))
                at = pl.ds(4 * p + 2 * t + h, PART, stride=12)
                keep_out[at, :] = jnp.where(left_core, a, b)
                send_out[at, :] = jnp.where(left_core, b, a)


def start_kernel(tile, probe, ob, pr, own):
    ob[:, :TILE, :TILE] = tile[...]
    pr[...] = probe[...]
    col = lax.axis_index("col")
    me = lax.axis_index("row") * (lax.axis_size("col") // 2) + col // 2
    row = lax.broadcasted_iota(jnp.int32, (F, LANES), 0)
    rows = []
    for p in range(2):
        for t in range(2):
            for h in range(2):
                picked = row == (2 * lax.rem(col, 2) + h) * PART + me
                rows.append(jnp.sum(jnp.where(picked, probe[p, :, t * LANES : (t + 1) * LANES], 0.0), axis=0, keepdims=True))
    own[...] = jnp.concatenate(rows, 0)


def first_kernel(mine, ia, ib, ic, amp, left, right, pr, tile, below, below_right, beside, corner, *rest):
    ob, light, outs, (unused, canvas, grads, listed, glow) = rest[0], rest[1], rest[2:9], rest[9:]
    ob[:, TILE:, :F] = below[...]
    ob[:, TILE:, F:TILE] = below_right[...]
    ob[:, :TILE, TILE:] = beside[...]
    ob[:, TILE:, TILE:] = corner[...]
    visit_frames(mine, (ia, ib, ic), amp, left, right, ob, pr, canvas, glow, grads, listed)
    light[...] = glow[F : F + WIDE, F : F + WIDE]
    hand_out(canvas, grads, *outs)


def gathered_probe(mine, other, pr):
    left_core = on_left_core()
    for p in range(2):
        for h in range(2):
            for t in range(2):
                at = pl.ds(4 * p + 2 * t + h, PART, stride=8)
                a, b = mine[at, :], other[at, :]
                for k in range(2):
                    rows = slice((2 * k + h) * PART, (2 * k + h + 1) * PART)
                    pr[p, rows, t * LANES : (t + 1) * LANES] = jnp.where(left_core == (k == 0), a, b)


def refreshed(put, size, o, l, zl, zr, up, mid, dn, left_in, right_in, across):
    for i in range(size // F):
        for j in range(size // F):
            for at in range(0, F, STRIP):
                here = slice(at, at + STRIP)
                rows, cols = slice(i * F + at, i * F + at + STRIP), slice(j * F, (j + 1) * F)
                scale = 1.0 / (l[rows, cols] + object_damping)
                for p in range(2):
                    if j == 0:
                        s = zl[p, rows, :] + left_in[p, rows, :]
                    elif j == 1:
                        s = (up, mid, dn)[i][p, here, :]
                    else:
                        s = zr[p, rows, :] + right_in[p, rows, :]
                    if i != 1:
                        s = s + across(i, j, p, here)
                    put(p, rows, cols, o[p, rows, cols] + s * scale)


def refresh_kernel(o, l, zl, zr, up, mid, dn, left_in, right_in, cup, cdn, sup, sdn, swap, ob):
    def put(p, rows, cols, value):
        ob[p, rows, cols] = value

    left_core = on_left_core()

    def across(i, j, p, here):
        centre, side = (cdn, sdn) if i == 0 else (cup, sup)
        if j == 1:
            return centre[p, here, :]
        outer = side[p, here, :]
        inner = centre[2, here, :] + swap[i // 2, here, :] if p == 0 else side[2, here, :]
        return jnp.where(left_core == (j == 2), inner, outer)

    refreshed(put, WIDE, o, l, zl, zr, up, mid, dn, left_in, right_in, across)


def next_kernel(mine, ia, ib, ic, amp, left, right, pg, po, ob, *rest):
    unused, light, outs, (pr, canvas, grads, listed, glow) = rest[0], rest[1], rest[2:9], rest[9:]
    gathered_probe(pg, po, pr)
    visit_frames(mine, (ia, ib, ic), amp, left, right, ob, pr, canvas, glow, grads, listed)
    light[...] = glow[F : F + WIDE, F : F + WIDE]
    hand_out(canvas, grads, *outs)


def last_kernel(o, l, zl, up, mid, left_in, cdn, sdn, o_out):
    def put(p, rows, cols, value):
        o_out[p, rows, cols] = value

    def across(i, j, p, here):
        return cdn[p, here, :] if j == 1 else sdn[0, p, here, :]

    refreshed(put, TILE, o, l, zl, None, up, mid, None, left_in, None, across)


def middle_kernel(last, g, old, zl, left_in, *rest):
    if last:
        sdn, new, spread = rest
        sdn[0] = zl[:, TILE:] + left_in[:, TILE:]
    else:
        zr, right_in, cup, cdn, sup, sdn, swap, new, spread = rest
        left_core = on_left_core()
        for out, rows in ((sup, slice(0, F)), (sdn, slice(TILE, WIDE))):
            for p in range(2):
                a = zl[p, rows] + left_in[p, rows]
                b = zr[p, rows] + right_in[p, rows]
                out[p] = jnp.where(left_core, a, b)
                if p == 1:
                    out[2] = jnp.where(left_core, b, a)
        swap[0] = cdn[2]
        swap[1] = cup[2]
    s = jnp.sum(g[...].reshape(PART // 2, 24, LANES), axis=0)
    s = s[:12] + s[12:]
    value = old[...] + s[:8] / (jnp.concatenate([s[8:], s[8:]], 0) + probe_damping)
    new[...] = value
    spread[...] = jnp.broadcast_to(value[None], (PART, 8, LANES)).reshape(PART * 8, LANES)


def f32(*shape):
    return jax.ShapeDtypeStruct(shape, jnp.float32)


def call(kernel, args, outs, scratch=(), limit=14, smem=(), cost=None, alias=None):
    return pl.pallas_call(
        kernel,
        out_shape=tuple(outs),
        in_specs=[SMEM if i in smem else VMEM for i in range(len(args))],
        out_specs=tuple(VMEM for _ in outs),
        scratch_shapes=list(scratch),
        compiler_params=pltpu.CompilerParams(vmem_limit_bytes=limit << 20),
        cost_estimate=cost,
        input_output_aliases=alias or {},
    )(*args)


def call_frames(kernel, *args, alias=None):
    scratch = [
        pltpu.VMEM((2, F, F), jnp.float32),
        pltpu.VMEM((2, WIDE, WIDE), jnp.float32),
        pltpu.VMEM((3, F, F), jnp.float32),
        pltpu.SMEM((2, 40), jnp.int32),
        pltpu.VMEM((WIDE + 2 * F, WIDE + 2 * F), jnp.float32),
    ]
    outs = (
        f32(2, WIDE, WIDE), f32(WIDE, WIDE), f32(2, WIDE, F), f32(2, WIDE, F),
        f32(3, F, F), f32(2, F, F), f32(3, F, F), f32(PART * 12, LANES), f32(PART * 12, LANES),
    )
    return call(kernel, args, outs, scratch, limit=FRAMES_LIMIT, smem=(0, 1, 2, 3), alias=alias)


def add_kernel(a, b, out):
    out[...] = a[...] + b[...]


def every_chip(x):
    size = lax.axis_size("row") * lax.axis_size("col")
    groups = [list(range(core, size, 2)) for core in range(2)]
    return lax.all_to_all(x, ("row", "col"), 0, 0, axis_index_groups=groups)


def other_core(x):
    return lax.ppermute(x, "col", [(i, i ^ 1) for i in range(lax.axis_size("col"))])


def shards(object_field, probe, amplitude, positions, counts):
    left, right = (jnp.asarray(t) for t in tables())
    amp = amplitude[0, 0]
    mine = jnp.concatenate([positions[0, 0, :, 0], positions[0, 0, :, 1], counts[0], jnp.zeros((7,), jnp.int32)])[None]

    below = passed_along(object_field[:, :F, :F], "row", -1)
    beside = passed_along(object_field[:, :, :F], "col", -1)
    below_right = passed_along(object_field[:, :F, F:], "row", -1)
    info = jnp.concatenate([passed_along(mine, "col", 1), mine, passed_along(mine, "col", -1)], 0)
    below, info = lax.optimization_barrier((below, info))
    infos = (passed_along(info, "row", 1), info, passed_along(info, "row", -1))
    corner = passed_along(below, "col", -1)
    wide, probe, own = call(start_kernel, (object_field, probe), (f32(2, WIDE, WIDE), f32(2, F, F), f32(8, LANES)))

    state = call_frames(
        first_kernel, mine, *infos, amp, left, right, probe, wide, below, below_right, beside, corner, alias={8: 0},
    )
    for sweep in range(PASSES):
        last = sweep == PASSES - 1
        ob, light, to_left, to_right, up, mid, down, keep, send = state
        grad = call(add_kernel, (keep, other_core(send)), (f32(PART * 12, LANES),))[0].reshape(PART, 3, 4, LANES)
        from_left = passed_along(to_right, "col", 1)
        centre_down = passed_along(down, "row", 1)
        moved = [from_left, centre_down]
        if not last:
            moved += [passed_along(to_left, "col", -1), passed_along(up, "row", -1)]
        grad, to_left, to_right = lax.optimization_barrier((grad, to_left, to_right))
        grad = every_chip(grad)
        grad, moved = lax.optimization_barrier((grad, moved))
        grad = grad.reshape(PART * 12, LANES)
        tail = (f32(8, LANES), f32(PART * 8, LANES))
        if last:
            from_left, centre_down = moved
            side_down, own, spread = call(
                lambda *refs: middle_kernel(True, *refs), (grad, own, to_left, from_left), (f32(1, 2, F, F),) + tail,
            )
            sides = (side_down,)
            moved = (passed_along(side_down, "row", 1),)
        else:
            from_left, centre_down, from_right, centre_up = moved
            side_up, side_down, swap, own, spread = call(
                lambda *refs: middle_kernel(False, *refs),
                (grad, own, to_left, from_left, to_right, from_right, centre_up, centre_down),
                (f32(3, F, F), f32(3, F, F), f32(2, F, F)) + tail,
            )
            sides = (side_up, side_down, swap)
            moved = (passed_along(side_up, "row", -1), passed_along(side_down, "row", 1), other_core(swap))
        sides, spread = lax.optimization_barrier((sides, spread))
        pg = every_chip(spread.reshape(PART, 2, 4, LANES)).reshape(PART * 8, LANES)
        po = other_core(pg)
        if last:
            object_out = call(
                last_kernel, (ob, light, to_left, up, mid, from_left, centre_down, moved[0]), (f32(2, TILE, TILE),),
            )[0]
            return object_out, call(gathered_probe, (pg, po), (f32(2, F, F),))[0]
        ob = call(
            refresh_kernel,
            (ob, light, to_left, to_right, up, mid, down, from_left, from_right, centre_up, centre_down, *moved),
            (f32(2, WIDE, WIDE),), alias={0: 0},
        )[0]
        state = call_frames(next_kernel, mine, *infos, amp, left, right, pg, po, ob, alias={9: 0})


def solution(mesh):
    return jax.shard_map(
        shards,
        mesh=mesh,
        in_specs=(
            P(None, "row", "col"),
            P(),
            P("row", "col", None, None, None),
            P("row", "col", None, None),
            P("row", "col"),
        ),
        out_specs=(P(None, "row", "col"), P()),
        check_vma=False,
    )
```
